32 devices in a mesh: seq: 16 (over z, y, x), mp: 2 (over core).
Axes of the slice: x: 2, y: 2, z: 4, core: 2. Of those that a mesh axis runs over, the one named last changes fastest.
Arguments:
- patch_states: bfloat16 [8192, 2048], P('seq'), may hold values from -6 to 6
- mlp_gain: bfloat16 [2048], replicated, may hold values from 0.099609375 to 1.8984375
- up_weight: bfloat16 [2048, 7168], P('seq', 'mp')
- down_weight: bfloat16 [7168, 2048], P('mp', 'seq')
- kv_gain: bfloat16 [2048], replicated, may hold values from 0.099609375 to 1.8984375
- kv_weight: bfloat16 [2048, 2048], P(None, 'mp'), may hold values from -0.125 to 0.125
- byte_states: bfloat16 [16384, 1024], P('seq'), may hold values from -6 to 6
- query_weight: bfloat16 [1024, 1024], P(None, 'mp'), may hold values from -0.1875 to 0.1875
- out_weight: bfloat16 [1024, 1024], P('mp'), may hold values from -0.75 to 0.75
- patch_counts: int32 [16], P('seq'), may hold values from 256 to 512, as said below
- byte_patch: int32 [16384], P('seq'), may hold values from 0 to 511, as said below
Outputs:
- decoded: bfloat16 [16384, 1024], P(('seq', 'mp'))
The draws below stay inside these ranges and needn't reach their ends.
Inputs may be any that keep to these rules, and one draw needn't show every extreme that they name: `patch_counts`: exactly 512 in some block and exactly 256 in another, in every draw. `byte_patch`: within each seq block of 1024 bytes the values start at 0, never fall, rise by at most one from one byte to the next, and end at that block's patch count minus one.
All inputs are finite; a program needn't handle non-finite values.
Results may differ from the reference program's by a relative error of at most 0.02.
Values may be sent and summed in bfloat16 or wider, within the bound.
A program may use at most 128 MiB of HBM per device.

```python
import math
import jax
import jax.numpy as jnp
from jax import lax

D = 2048
FF = 7168
HEADS = 8
HS = 128
WIN = 1024
PATCH_DEV = 512
BYTE_DEV = 1024
DL = 1024
HALO = 4
NP = 8192
NB = 16384
N_MP = 2


def shuffled_slots(one_key):
    return jax.random.permutation(one_key, BYTE_DEV - 1)


def patch_layout(key):
    shard_total = NP // PATCH_DEV
    base = jax.random.fold_in(key, 11)
    count_key, pick_key, cut_key = jax.random.split(base, 3)
    counts = jax.random.randint(count_key, (shard_total,), PATCH_DEV // 2, PATCH_DEV + 1).astype(jnp.int32)
    order = jax.random.permutation(pick_key, shard_total)
    counts = counts.at[order[0]].set(PATCH_DEV).at[order[1]].set(PATCH_DEV // 2)
    cut_keys = jax.random.split(cut_key, shard_total)
    ranks = jax.vmap(shuffled_slots)(cut_keys)
    starts = (ranks < counts[:, None] - 1).astype(jnp.int32)
    byte_patch = jnp.concatenate([jnp.zeros((shard_total, 1), jnp.int32), jnp.cumsum(starts, axis=1).astype(jnp.int32)], axis=1)
    return (counts.astype(jnp.int32), byte_patch.reshape(shard_total * BYTE_DEV).astype(jnp.int32))


def draw_patch_counts(key, part):
    return patch_layout(key)[0]


def draw_byte_patch(key, part):
    return patch_layout(key)[1]


def group_weight(key, shape, tile_axis, fan_in):
    width = FF // N_MP
    if tile_axis == 1:
        common_shape = (shape[0], width)
        repeats = (1, N_MP)
    else:
        common_shape = (width, shape[1])
        repeats = (N_MP, 1)
    shared_key, own_key = jax.random.split(jax.random.fold_in(key, 29))
    shared = jnp.clip(jax.random.normal(shared_key, common_shape, jnp.float32), -4.0, 4.0)
    own_part = jnp.clip(jax.random.normal(own_key, shape, jnp.float32), -4.0, 4.0)
    shared_mix = 0.7071068
    own_mix = 0.7071068
    tiled = jnp.tile(shared, repeats)
    mixed_values = (shared_mix * tiled + own_mix * own_part) * float(fan_in) ** (-0.5)
    return mixed_values.astype(jnp.float32).astype(jnp.bfloat16)


def draw_up_weight(key, part):
    return group_weight(jax.random.fold_in(key, 41), (D, FF), 1, D)


def draw_down_weight(key, part):
    return group_weight(jax.random.fold_in(key, 53), (FF, D), 0, FF)


def levels(rng, shape, cuts, least, high):
    factor_of, own = 1.0, jax.random.fold_in(rng, 6)
    for position, shards_of in cuts:
        steps = jnp.exp(jax.random.uniform(jax.random.fold_in(own, position), (shards_of,), jnp.float32, least / len(cuts), high / len(cuts)))
        factor_of = factor_of * jnp.repeat(steps, shape[position] // shards_of).reshape([-1 if axis == position else 1 for axis in range(len(shape))])
    return factor_of


def noise(rng, dims, scale, limit, cuts=(), kind=jnp.bfloat16):
    level = levels(rng, dims, cuts, -0.22, 0.18) if cuts else 1.0
    drawn = jax.random.normal(rng, dims, jnp.float32) * scale * level
    return jnp.minimum(jnp.maximum(drawn, -limit), limit).astype(kind)


def setup_inputs(seed: int = 0) -> dict:
    key_list = jax.random.split(jax.random.key(seed), 12)
    return {
        "patch_states": noise(key_list[0], (NP, D), 1.0, 6.0, ((0, 16),)),
        "mlp_gain": jnp.clip(1.0 + 0.18 * jax.random.normal(key_list[1], (D,), jnp.float32), 0.099609375, 1.8984375).astype(jnp.bfloat16),
        "up_weight": draw_up_weight(jax.random.fold_in(key_list[11], 71), 0),
        "down_weight": draw_down_weight(jax.random.fold_in(key_list[11], 71), 0),
        "kv_gain": jnp.clip(1.0 + 0.18 * jax.random.normal(key_list[4], (D,), jnp.float32), 0.099609375, 1.8984375).astype(jnp.bfloat16),
        "kv_weight": noise(key_list[5], (D, 2 * DL), D ** -0.5, 0.125, ((1, 2),)),
        "byte_states": noise(key_list[6], (NB, DL), 1.0, 6.0, ((0, 16),)),
        "query_weight": noise(key_list[7], (DL, DL), DL ** -0.5, 0.1875, ((1, 2),)),
        "out_weight": noise(key_list[8], (DL, DL), (DL // 16) ** -0.5, 0.75, ((0, 2),)),
        "patch_counts": draw_patch_counts(jax.random.fold_in(key_list[11], 71), 0),
        "byte_patch": draw_byte_patch(jax.random.fold_in(key_list[11], 71), 0),
    }


def scale_rows(values, gain):
    return values * lax.rsqrt(lax.optimization_barrier(jnp.mean(values * values, axis=-1, keepdims=True)) + 1e-05) * gain

def unit_rows(values):
    return values * lax.rsqrt(lax.optimization_barrier(jnp.mean(values * values, axis=-1, keepdims=True)) + 1e-06)

def reference(patch_states, mlp_gain, up_weight, down_weight, kv_gain, kv_weight, byte_states, query_weight, out_weight, patch_counts, byte_patch):
    shards = patch_counts.shape[0]
    group_width = FF // N_MP

    def patch_block(rows):
        normed = scale_rows(rows.astype(jnp.float32), mlp_gain.astype(jnp.float32)).astype(jnp.bfloat16)
        preact = jnp.dot(normed, up_weight, preferred_element_type=jnp.float32)
        hidden = jax.nn.gelu(preact, approximate=False).astype(jnp.bfloat16)
        mixed_out = jnp.zeros(rows.shape, jnp.float32)
        for group_index in range(N_MP):
            lower = group_index * group_width
            upper = lower + group_width
            piece_sum = jnp.dot(hidden[:, lower:upper], down_weight[lower:upper], preferred_element_type=jnp.float32)
            rounded = lax.optimization_barrier(piece_sum.astype(jnp.bfloat16))
            mixed_out = mixed_out + rounded.astype(jnp.float32)
        kv_in = scale_rows(rows.astype(jnp.float32) + mixed_out, kv_gain.astype(jnp.float32)).astype(jnp.bfloat16)
        projected = jnp.dot(kv_in, kv_weight, preferred_element_type=jnp.float32).reshape(rows.shape[0], HEADS, 2, HS)
        keys = unit_rows(projected[:, :, 0])
        return jnp.stack([keys, projected[:, :, 1]], axis=2).astype(jnp.bfloat16)
    packed = lax.map(patch_block, patch_states.reshape(shards, PATCH_DEV, D))
    queries = unit_rows(jnp.dot(byte_states, query_weight, preferred_element_type=jnp.float32).reshape(shards, BYTE_DEV, HEADS, HS)).astype(jnp.bfloat16)
    counts = patch_counts.astype(jnp.int32)
    offsets = (jnp.cumsum(counts) - counts).astype(jnp.int32)
    padded = jnp.concatenate([jnp.zeros((HALO,) + packed.shape[1:], jnp.bfloat16), packed], axis=0)
    head_group = HEADS // N_MP
    score_scale = 2.0 / math.sqrt(HS)

    def shard_out(inputs):
        shard_index, shard_queries, shard_bytes = inputs
        slab = lax.dynamic_slice_in_dim(padded, shard_index.astype(jnp.int32), HALO + 1, 0)
        shard_ids = (shard_index - HALO + jnp.arange(HALO + 1, dtype=jnp.int32)).astype(jnp.int32)
        present = shard_ids >= 0
        safe_ids = jnp.clip(shard_ids, 0, shards - 1).astype(jnp.int32)
        first_ids = jnp.where(present, offsets[safe_ids], 0).astype(jnp.int32)
        live_counts = jnp.where(present, counts[safe_ids], 0).astype(jnp.int32)
        positions = jnp.arange(PATCH_DEV, dtype=jnp.int32)
        key_ids = (first_ids[:, None] + positions[None, :]).reshape(-1)
        live_mask = (positions[None, :] < live_counts[:, None]).reshape(-1)
        own_patch = (offsets[shard_index] + shard_bytes).astype(jnp.int32)
        usable = live_mask[None, :] & (key_ids[None, :] <= own_patch[:, None]) & (key_ids[None, :] > own_patch[:, None] - WIN)
        keys = slab[:, :, :, 0].reshape((HALO + 1) * PATCH_DEV, HEADS, HS)
        values = slab[:, :, :, 1].reshape((HALO + 1) * PATCH_DEV, HEADS, HS)
        scores = jnp.einsum('bhd,khd->hbk', shard_queries.astype(jnp.float32), keys.astype(jnp.float32)) * score_scale
        weights = jnp.where(usable[None], jnp.exp(scores), 0.0)
        rounded_weights = lax.optimization_barrier(weights.astype(jnp.bfloat16)).astype(jnp.float32)
        numerator = jnp.einsum('hbk,khd->bhd', rounded_weights, values.astype(jnp.float32))
        denominator = lax.optimization_barrier(jnp.sum(weights, axis=-1))
        attended = (numerator / jnp.transpose(denominator)[:, :, None]).astype(jnp.bfloat16).reshape(BYTE_DEV, HEADS * HS)
        total = jnp.zeros((BYTE_DEV, HEADS * HS), jnp.float32)
        for group_index in range(N_MP):
            lower = group_index * head_group * HS
            upper = lower + head_group * HS
            piece_sum = jnp.dot(attended[:, lower:upper], out_weight[lower:upper], preferred_element_type=jnp.float32)
            rounded = lax.optimization_barrier(piece_sum.astype(jnp.bfloat16))
            total = total + rounded.astype(jnp.float32)
        return total.astype(jnp.bfloat16)
    outputs = lax.map(shard_out, (jnp.arange(shards, dtype=jnp.int32), queries, byte_patch.reshape(shards, BYTE_DEV)))
    return outputs.reshape(shards * BYTE_DEV, HEADS * HS)
```

```python
import functools
import math

import jax
import jax.numpy as jnp
from jax import lax
from jax.experimental import pallas as pl
from jax.experimental.pallas import tpu as pltpu
from jax.sharding import PartitionSpec as P

HS = 128
WIN = 1024
KEY_TILE = 256


def scale_rows(values, gain):
    return values * lax.rsqrt(jnp.mean(values * values, axis=-1, keepdims=True) + 1e-05) * gain


def unit_rows(values):
    return values * lax.rsqrt(jnp.mean(values * values, axis=-1, keepdims=True) + 1e-06)


def sum_over_cores(value, scatter_dim):
    count = lax.axis_size("mp")
    if count != 2:
        return lax.psum_scatter(value, "mp", scatter_dimension=scatter_dim, tiled=True).astype(
            jnp.float32
        )
    me = lax.axis_index("mp")
    width = value.shape[scatter_dim] // 2
    theirs = lax.dynamic_slice_in_dim(value, (1 - me) * width, width, scatter_dim)
    mine = lax.dynamic_slice_in_dim(value, me * width, width, scatter_dim)
    got = lax.ppermute(theirs, "mp", [(0, 1), (1, 0)])
    return mine.astype(jnp.float32) + got.astype(jnp.float32)


def join_cores(value, dim):
    count = lax.axis_size("mp")
    if count != 2:
        return lax.all_gather(value, "mp", axis=dim, tiled=True)
    me = lax.axis_index("mp")
    got = lax.ppermute(value, "mp", [(0, 1), (1, 0)])
    first = jnp.where(me == 0, value, got)
    second = jnp.where(me == 0, got, value)
    return jnp.concatenate([first, second], axis=dim)


def attend_kernel(heads, distances, start, finish, scalars, ends, query, byte_patch, *refs):
    kv_refs, refs = refs[: len(distances)], refs[len(distances) :]
    if not start:
        (num_in, den_in), refs = refs[:2], refs[2:]
    if finish:
        out_weight, out, num, den = refs
    else:
        num, den = refs
    if start:
        num[...] = jnp.zeros_like(num)
        den[...] = jnp.zeros_like(den)
    else:
        num[...] = num_in[...]
        den[...] = den_in[...]
    tile = pl.program_id(0)
    lowest, highest = ends[2 * tile], ends[2 * tile + 1]
    scale = 2.0 / math.sqrt(HS) * math.log2(math.e)
    for distance, kv_ref in zip(distances, kv_refs):
        first, live = scalars[2 * distance], scalars[2 * distance + 1]
        for low in range(0, kv_ref.shape[0], KEY_TILE):
            last = first + jnp.minimum(live, low + KEY_TILE) - 1
            seen = (low < live) & (first + low <= highest) & (last > lowest - WIN)

            @pl.when(seen)
            def _(kv_ref=kv_ref, low=low, first=first, live=live):
                rows = query.shape[0]
                position = low + lax.broadcasted_iota(jnp.int32, (rows, KEY_TILE), 1)
                gap = byte_patch[...] - first - position
                usable = (position < live) & (gap >= 0) & (gap < WIN)
                for head in range(heads):
                    columns = slice(head * HS, (head + 1) * HS)
                    key = kv_ref[low : low + KEY_TILE, head * 2 * HS : head * 2 * HS + HS]
                    value = kv_ref[low : low + KEY_TILE, head * 2 * HS + HS : (head + 1) * 2 * HS]
                    scores = lax.dot_general(
                        query[:, columns],
                        key,
                        (((1,), (1,)), ((), ())),
                        preferred_element_type=jnp.float32,
                    )
                    weights = jnp.where(usable, jnp.exp2(scores * scale), 0.0)
                    den[:, columns] += weights[:, :HS] + weights[:, HS:]
                    num[:, columns] += jnp.dot(
                        weights.astype(jnp.bfloat16), value, preferred_element_type=jnp.float32
                    )

    if finish:
        parts = []
        for head in range(heads):
            columns = slice(head * HS, (head + 1) * HS)
            total = jnp.sum(den[:, columns], axis=1, keepdims=True)
            parts.append((num[:, columns] / total).astype(jnp.bfloat16))
        attended = jnp.concatenate(parts, axis=1)
        out[...] = jnp.dot(
            attended, out_weight[...], preferred_element_type=jnp.float32
        ).astype(jnp.bfloat16)


def attend(distances, scalars, ends, query, byte_patch, blocks, sums=None, out_weight=None):
    rows, width = query.shape
    heads = width // HS
    tile = rows // (ends.shape[0] // 2)
    start, finish = sums is None, out_weight is not None
    smem = pl.BlockSpec(memory_space=pltpu.SMEM)
    tiled = lambda columns: pl.BlockSpec((tile, columns), lambda i: (i, 0))
    whole = lambda array: pl.BlockSpec(array.shape, lambda i: (0, 0))
    operands = [scalars, ends, query, byte_patch, *blocks]
    in_specs = [smem, smem, tiled(width), tiled(1)] + [whole(block) for block in blocks]
    if not start:
        operands += list(sums)
        in_specs += [tiled(width), tiled(width)]
    if finish:
        operands.append(out_weight)
        in_specs.append(whole(out_weight))
        out_shape = jax.ShapeDtypeStruct((rows, out_weight.shape[1]), jnp.bfloat16)
        out_specs = tiled(out_weight.shape[1])
        scratch = [pltpu.VMEM((tile, width), jnp.float32)] * 2
    else:
        out_shape = [jax.ShapeDtypeStruct((rows, width), jnp.float32)] * 2
        out_specs = [tiled(width)] * 2
        scratch = []
    keys = sum(block.shape[0] for block in blocks)
    return pl.pallas_call(
        functools.partial(attend_kernel, heads, distances, start, finish),
        grid=(rows // tile,),
        in_specs=in_specs,
        out_specs=out_specs,
        out_shape=out_shape,
        scratch_shapes=scratch,
        compiler_params=pltpu.CompilerParams(vmem_limit_bytes=48 * 2**20),
        cost_estimate=pl.CostEstimate(
            flops=8 * rows * keys * width, bytes_accessed=4 * keys * width, transcendentals=0
        ),
    )(*operands)


def on_device(
    patch_states,
    mlp_gain,
    up_weight,
    down_weight,
    kv_gain,
    kv_weight,
    byte_states,
    query_weight,
    out_weight,
    patch_counts,
    byte_patch,
):
    seq = lax.axis_size("seq")
    me = lax.axis_index("seq")
    patch_rows, features = patch_states.shape
    size = 4 if seq % 4 == 0 else 1
    groups = [[base + i for i in range(size)] for base in range(0, seq, size)]
    across = [[base + i for base in range(0, seq, size)] for i in range(size)]
    place = lax.rem(me, size)

    up_part = lax.all_to_all(up_weight, "seq", 1, 0, axis_index_groups=groups, tiled=True)
    down_part = lax.all_to_all(down_weight, "seq", 0, 1, axis_index_groups=groups, tiled=True)
    up_all = lax.all_gather(up_part, "seq", axis=0, tiled=True, axis_index_groups=across)
    down_all = lax.all_gather(down_part, "seq", axis=1, tiled=True, axis_index_groups=across)

    normed = scale_rows(patch_states.astype(jnp.float32), mlp_gain.astype(jnp.float32)).astype(
        jnp.bfloat16
    )
    tokens = lax.all_gather(normed, "seq", axis=0, tiled=True, axis_index_groups=groups)
    counts = lax.all_gather(patch_counts, "seq", axis=0, tiled=True)

    heads_here = kv_weight.shape[1] // (2 * HS)
    bytes_here = byte_states.shape[0]
    query_proj = jnp.dot(byte_states, query_weight, preferred_element_type=jnp.float32).reshape(
        bytes_here, heads_here, HS
    )
    queries = unit_rows(query_proj).astype(jnp.bfloat16).reshape(bytes_here, heads_here * HS)

    preact = jnp.dot(tokens, up_all, preferred_element_type=jnp.float32)
    hidden = jax.nn.gelu(preact, approximate=False).astype(jnp.bfloat16)
    partial_value = jnp.dot(hidden, down_all, preferred_element_type=jnp.float32).astype(
        jnp.bfloat16
    )
    part = sum_over_cores(partial_value, 1).astype(jnp.bfloat16)
    part = part.reshape(size, patch_rows, part.shape[1])
    mixed = lax.dynamic_index_in_dim(part, place, 0, keepdims=False).astype(jnp.float32)
    for turn in range(1, size):
        pairs = [(base + i, base + (i ^ turn)) for base in range(0, seq, size) for i in range(size)]
        piece = lax.dynamic_index_in_dim(part, lax.bitwise_xor(place, turn), 0, keepdims=False)
        mixed = mixed + lax.ppermute(piece, "seq", pairs).astype(jnp.float32)
    mixed = join_cores(mixed.astype(jnp.bfloat16), 1).astype(jnp.float32)

    kv_in = scale_rows(
        patch_states.astype(jnp.float32) + mixed, kv_gain.astype(jnp.float32)
    ).astype(jnp.bfloat16)
    projected = jnp.dot(kv_in, kv_weight, preferred_element_type=jnp.float32).reshape(
        patch_rows, heads_here, 2, HS
    )
    kv_pack = (
        jnp.stack([unit_rows(projected[:, :, 0]), projected[:, :, 1]], axis=2)
        .astype(jnp.bfloat16)
        .reshape(patch_rows, heads_here * 2 * HS)
    )

    fewest = patch_rows // 2
    depth = (WIN + fewest - 2) // fewest
    own_count = patch_counts[0]
    blocks = [kv_pack]
    scalars = [jnp.zeros((), jnp.int32), own_count]
    first = jnp.zeros((), jnp.int32)
    for back in range(1, depth + 1):
        need = min(patch_rows, -(-(WIN - 1 - (back - 1) * fewest) // KEY_TILE) * KEY_TILE)
        source = kv_pack
        if need <= fewest:
            source = lax.dynamic_slice_in_dim(kv_pack, own_count - need, need, 0)
        blocks.append(
            lax.ppermute(source, "seq", [(i, i + back) for i in range(max(0, seq - back))])
        )
        held = jnp.where(me >= back, counts[jnp.maximum(me - back, 0)], 0)
        first = first - held
        if need <= fewest:
            scalars += [first + held - need, jnp.where(me >= back, need, 0)]
        else:
            scalars += [first, held]
    scalars = jnp.stack(scalars).astype(jnp.int32)
    tile = min(256, bytes_here)
    by_tile = byte_patch.reshape(bytes_here // tile, tile)
    ends = jnp.stack([by_tile[:, 0], by_tile[:, -1]], axis=1).reshape(-1)
    columns = byte_patch[:, None]
    sums = attend((0,), scalars, ends, queries, columns, blocks[:1])
    for back in range(1, depth):
        sums = attend((back,), scalars, ends, queries, columns, blocks[back : back + 1], sums)
    term = attend((depth,), scalars, ends, queries, columns, blocks[depth:], sums, out_weight)
    return sum_over_cores(term, 0).astype(jnp.bfloat16)


def solution(mesh):
    in_specs = (
        P("seq", None),
        P(),
        P("seq", "mp"),
        P("mp", "seq"),
        P(),
        P(None, "mp"),
        P("seq", None),
        P(None, "mp"),
        P("mp", None),
        P("seq"),
        P("seq"),
    )
    out_specs = P(("seq", "mp"), None)
    return jax.shard_map(
        on_device, mesh=mesh, in_specs=in_specs, out_specs=out_specs, check_vma=False
    )
```

```python
import functools
import math

import jax
import jax.numpy as jnp
from jax import lax
from jax.experimental import pallas as pl
from jax.experimental.pallas import tpu as pltpu
from jax.sharding import PartitionSpec as P

HS = 128
WIN = 1024
KEY_TILE = 256
PLANE = 4
TILE = 128


def scale_rows(values, gain):
    return values * lax.rsqrt(jnp.mean(values * values, axis=-1, keepdims=True) + 1e-05) * gain


def unit_rows(values):
    return values * lax.rsqrt(jnp.mean(values * values, axis=-1, keepdims=True) + 1e-06)


def sum_over_cores(value, scatter_dim):
    count = lax.axis_size("mp")
    if count != 2:
        return lax.psum_scatter(value, "mp", scatter_dimension=scatter_dim, tiled=True).astype(
            jnp.float32
        )
    me = lax.axis_index("mp")
    width = value.shape[scatter_dim] // 2
    theirs = lax.dynamic_slice_in_dim(value, (1 - me) * width, width, scatter_dim)
    mine = lax.dynamic_slice_in_dim(value, me * width, width, scatter_dim)
    got = lax.ppermute(theirs, "mp", [(0, 1), (1, 0)])
    return mine.astype(jnp.float32) + got.astype(jnp.float32)


def join_cores(value, dim):
    count = lax.axis_size("mp")
    if count != 2:
        return lax.all_gather(value, "mp", axis=dim, tiled=True)
    me = lax.axis_index("mp")
    got = lax.ppermute(value, "mp", [(0, 1), (1, 0)])
    first = jnp.where(me == 0, value, got)
    second = jnp.where(me == 0, got, value)
    return jnp.concatenate([first, second], axis=dim)


def block_kernel(
    patch, mlp_gain, up, down, kv_gain, kv_weight, byte_states, query_weight,
    kv_out, query_out,
    up_all, down_all, tokens, hidden, core_send, core_got, kept, plane_send, plane_got, mixed,
    swap_send, swap_recv, chunk_recv, right_send, left_send,
    token_send, token_recv, half_send, half_recv,
    core_sems, plane_sems, plane_recv, mixed_send, mixed_recv, local_sems,
):
    seq, core = lax.axis_index("seq"), lax.axis_index("mp")
    depth = lax.axis_size("seq") // PLANE
    z, place = seq // PLANE, lax.rem(seq, PLANE)
    y, x = place // 2, lax.rem(place, 2)
    rows, features = patch.shape
    thin = up.shape[0]
    units = up_all.shape[1]
    half = features // 2
    wide = features // (2 * depth)
    MESH = pl.DeviceIdType.MESH

    def member(turn):
        return 2 * lax.rem(y + turn // 2, 2) + lax.rem(x + lax.rem(turn, 2), 2)

    def peer(turn):
        return (z * PLANE + member(turn), core)

    partner = (seq, 1 - core)

    barrier = pltpu.get_barrier_semaphore()
    for turn in range(1, PLANE):
        pl.semaphore_signal(barrier, inc=1, device_id=peer(turn), device_id_type=MESH)
    pl.semaphore_signal(barrier, inc=1, device_id=partner, device_id_type=MESH)

    @pl.when(z > 0)
    def _():
        pl.semaphore_signal(barrier, inc=1, device_id=(seq - PLANE, core), device_id_type=MESH)

    @pl.when(z < depth - 1)
    def _():
        pl.semaphore_signal(barrier, inc=1, device_id=(seq + PLANE, core), device_id_type=MESH)

    pl.semaphore_wait(
        barrier, PLANE + jnp.where(z > 0, 1, 0) + jnp.where(z < depth - 1, 1, 0)
    )

    def remote(src, dst, send, recv, device):
        return pltpu.make_async_remote_copy(
            src_ref=src, dst_ref=dst, send_sem=send, recv_sem=recv, device_id=device,
            device_id_type=MESH,
        )

    def chunk(kind, index):
        if kind == 0:
            return up_all.at[pl.ds(pl.multiple_of(index * thin, thin), thin), :]
        return down_all.at[index]

    def held(kind, owner):
        start = pl.multiple_of(owner * units, units)
        if kind == 0:
            return up.at[:, pl.ds(start, units)]
        return down.at[pl.ds(start, units), :]

    def swap(kind, turn):
        index = z * PLANE + place
        return remote(
            held(kind, member(turn)), chunk(kind, index), swap_send.at[kind, turn],
            swap_recv.at[kind, turn], peer(turn),
        )

    def swap_arrives(kind, turn):
        index = z * PLANE + member(turn)
        return remote(
            chunk(kind, index), chunk(kind, index), swap_send.at[kind, turn],
            swap_recv.at[kind, turn], peer(turn),
        )

    def pass_right(kind, index):
        return remote(
            chunk(kind, index), chunk(kind, index), right_send.at[kind, index],
            chunk_recv.at[kind, index], (seq + PLANE, core),
        )

    def pass_left(kind, index):
        return remote(
            chunk(kind, index), chunk(kind, index), left_send.at[kind, index],
            chunk_recv.at[kind, index], (seq - PLANE, core),
        )

    def spread(kind, index):
        @pl.when(z < depth - 1)
        def _():
            pass_right(kind, index).start()

        @pl.when(z > 0)
        def _():
            pass_left(kind, index).start()

    def hop(kind, step):
        far, turn = step // PLANE, lax.rem(step, PLANE)

        @pl.when(z - 1 - far >= 0)
        def _():
            index = (z - 1 - far) * PLANE + member(turn)
            pass_left(kind, index).wait_recv()

            @pl.when(z < depth - 1)
            def _():
                pass_right(kind, index).start()

        @pl.when(z + 1 + far < depth)
        def _():
            index = (z + 1 + far) * PLANE + member(turn)
            pass_right(kind, index).wait_recv()

            @pl.when(z > 0)
            def _():
                pass_left(kind, index).start()

    own = [
        pltpu.make_async_copy(held(kind, place), chunk(kind, seq), local_sems.at[kind])
        for kind in range(2)
    ]
    for kind in range(2):
        own[kind].start()
    for turn in range(1, PLANE):
        swap(0, turn).start()
    own[0].wait()
    spread(0, seq)

    gain = mlp_gain[...].astype(jnp.float32)
    row_start = pl.multiple_of(place * rows, rows)

    @pl.loop(0, rows // TILE)
    def _(tile):
        low = pl.multiple_of(tile * TILE, TILE)
        values = patch[pl.ds(low, TILE), :].astype(jnp.float32)
        tokens[pl.ds(row_start + low, TILE), :] = scale_rows(values, gain).astype(jnp.bfloat16)

    for turn in range(1, PLANE):
        swap_arrives(0, turn).wait_recv()
        spread(0, z * PLANE + member(turn))
    for turn in range(1, PLANE):
        swap(1, turn).start()

    def token_part(owner, side):
        return tokens.at[
            pl.ds(pl.multiple_of(owner * rows, rows), rows),
            pl.ds(pl.multiple_of(side * half, half), half),
        ]

    def send_tokens(turn):
        return remote(
            token_part(place, core), token_part(place, core), token_send.at[turn],
            token_recv.at[turn], peer(turn),
        )

    def tokens_arrive(turn):
        part = token_part(member(turn), core)
        return remote(part, part, token_send.at[turn], token_recv.at[turn], peer(turn))

    def half_over(turn):
        part = token_part(member(turn), core)
        return remote(part, part, half_send.at[turn], half_recv.at[turn], partner)

    def half_arrives(turn):
        part = token_part(member(turn), 1 - core)
        return remote(part, part, half_send.at[turn], half_recv.at[turn], partner)

    for turn in range(1, PLANE):
        send_tokens(turn).start()

    heads = query_weight.shape[1] // HS
    query_rows = byte_states.shape[0] // PLANE

    @pl.loop(0, PLANE)
    def _(step):
        low = pl.multiple_of(step * query_rows, query_rows)
        product = jnp.dot(
            byte_states[pl.ds(low, query_rows), :], query_weight[...],
            preferred_element_type=jnp.float32,
        )
        for head in range(heads):
            columns = slice(head * HS, (head + 1) * HS)
            query_out[pl.ds(low, query_rows), columns] = unit_rows(product[:, columns]).astype(
                jnp.bfloat16
            )
        hop(0, step)

    own[1].wait()
    spread(1, seq)
    for turn in range(1, PLANE):
        swap_arrives(1, turn).wait_recv()
        spread(1, z * PLANE + member(turn))

    @pl.loop(PLANE, 2 * PLANE)
    def _(step):
        hop(0, step)

    for turn in range(1, PLANE):
        tokens_arrive(turn).wait_recv()
        half_over(turn).start()

    @pl.loop(2 * PLANE, (depth - 1) * PLANE)
    def _(step):
        hop(0, step)

    for turn in range(1, PLANE):
        half_arrives(turn).wait_recv()

    tall = PLANE * rows // (2 * PLANE)

    @pl.loop(0, 2 * PLANE)
    def _(step):
        low = pl.multiple_of(step * tall, tall)
        preact = jnp.dot(
            tokens[pl.ds(low, tall), :], up_all[...], preferred_element_type=jnp.float32
        )
        gelu = 0.5 * preact * (1.0 + lax.erf(preact * math.sqrt(0.5)))
        hidden[pl.ds(low, tall), :] = gelu.astype(jnp.bfloat16)
        hop(1, step)

    near = jnp.minimum(z, depth - 1 - z)

    def order(turn):
        swapped = jnp.where((near == 1) & (turn < 2), 1 - turn, turn)
        return jnp.where(z < depth // 2, swapped, depth - 1 - swapped)

    def plane_out(turn, to):
        start = pl.multiple_of(member(to) * rows, rows)
        return remote(
            plane_send.at[turn, pl.ds(start, rows), :], plane_got.at[turn, to],
            plane_sems.at[turn, to], plane_recv.at[turn, to], peer(to),
        )

    def core_swap(turn):
        return remote(
            core_send, core_got.at[turn], core_sems.at[0, turn], core_sems.at[1, turn], partner
        )

    def product(turn, side, out):
        chunks = order(turn) * PLANE + side * (PLANE // 2)
        weight = jnp.concatenate([down_all[chunks + i] for i in range(PLANE // 2)], axis=1)

        @pl.loop(0, PLANE)
        def _(owner):
            low = pl.multiple_of(owner * rows, rows)
            out[pl.ds(low, rows), :] = jnp.dot(
                hidden[pl.ds(low, rows), :], weight, preferred_element_type=jnp.float32
            ).astype(jnp.bfloat16)

    def one_block(turn):
        product(turn, 1 - core, core_send)
        core_swap(turn).start()
        product(turn, core, kept)
        core_swap(turn).wait()

        @pl.loop(0, PLANE)
        def _(owner):
            low = pl.multiple_of(owner * rows, rows)
            total = kept[pl.ds(low, rows), :].astype(jnp.float32) + core_got[
                turn, pl.ds(low, rows), :
            ].astype(jnp.float32)
            plane_send[turn, pl.ds(low, rows), :] = total.astype(jnp.bfloat16)

        for to in range(1, PLANE):
            plane_out(turn, to).start()

    @pl.loop(0, depth - 1)
    def _(turn):
        one_block(turn)

    @pl.loop(2 * PLANE, (depth - 1) * PLANE)
    def _(step):
        hop(1, step)

    one_block(depth - 1)

    def mixed_over(turn, side):
        part = mixed.at[2 * order(turn) + side]
        return remote(part, part, mixed_send.at[turn], mixed_recv.at[turn], partner)

    @pl.loop(0, depth)
    def _(turn):
        total = plane_send[turn, pl.ds(row_start, rows), :].astype(jnp.float32)
        for to in range(1, PLANE):
            plane_out(turn, to).wait_recv()
            total = total + plane_got[turn, to].astype(jnp.float32)
        mixed[2 * order(turn) + core] = total.astype(jnp.bfloat16)
        mixed_over(turn, core).start()

    @pl.loop(0, depth)
    def _(turn):
        mixed_over(turn, 1 - core).wait_recv()

    later_gain = kv_gain[...].astype(jnp.float32)

    @pl.loop(0, rows // TILE)
    def _(tile):
        low = pl.multiple_of(tile * TILE, TILE)
        more = jnp.concatenate(
            [mixed[i, pl.ds(low, TILE), :] for i in range(2 * depth)], axis=1
        )
        values = patch[pl.ds(low, TILE), :].astype(jnp.float32) + more.astype(jnp.float32)
        kv_in = scale_rows(values, later_gain).astype(jnp.bfloat16)
        projected = jnp.dot(kv_in, kv_weight[...], preferred_element_type=jnp.float32)
        for head in range(heads):
            key = slice(head * 2 * HS, head * 2 * HS + HS)
            value = slice(head * 2 * HS + HS, (head + 1) * 2 * HS)
            kv_out[pl.ds(low, TILE), key] = unit_rows(projected[:, key]).astype(jnp.bfloat16)
            kv_out[pl.ds(low, TILE), value] = projected[:, value].astype(jnp.bfloat16)

    for turn in range(1, PLANE):
        for kind in range(2):
            swap(kind, turn).wait_send()
        send_tokens(turn).wait_send()
        half_over(turn).wait_send()

    @pl.loop(0, depth)
    def _(turn):
        for to in range(1, PLANE):
            plane_out(turn, to).wait_send()
        mixed_over(turn, core).wait_send()

    @pl.loop(0, depth * PLANE)
    def _(index):
        @pl.when((z < depth - 1) & (index // PLANE <= z))
        def _():
            for kind in range(2):
                pass_right(kind, index).wait_send()

        @pl.when((z > 0) & (index // PLANE >= z))
        def _():
            for kind in range(2):
                pass_left(kind, index).wait_send()


def patch_block(
    patch, mlp_gain, up, down, kv_gain, kv_weight, byte_states, query_weight, depth
):
    rows, features = patch.shape
    thin = up.shape[0]
    units = up.shape[1] // PLANE
    wide = features // (2 * depth)
    vmem = pl.BlockSpec(memory_space=pltpu.VMEM)
    bf16 = lambda *shape: pltpu.VMEM(shape, jnp.bfloat16)
    dma = lambda *shape: pltpu.SemaphoreType.DMA(shape)
    return pl.pallas_call(
        block_kernel,
        in_specs=[vmem] * 8,
        out_specs=[vmem] * 2,
        out_shape=[
            jax.ShapeDtypeStruct((rows, kv_weight.shape[1]), jnp.bfloat16),
            jax.ShapeDtypeStruct((byte_states.shape[0], query_weight.shape[1]), jnp.bfloat16),
        ],
        scratch_shapes=[
            bf16(features, units),
            bf16(depth * PLANE, units, thin),
            bf16(PLANE * rows, features),
            bf16(PLANE * rows, units),
            bf16(PLANE * rows, wide),
            bf16(depth, PLANE * rows, wide),
            bf16(PLANE * rows, wide),
            bf16(depth, PLANE * rows, wide),
            bf16(depth, PLANE, rows, wide),
            bf16(2 * depth, rows, wide),
            dma(2, PLANE), dma(2, PLANE), dma(2, depth * PLANE),
            dma(2, depth * PLANE), dma(2, depth * PLANE),
            dma(PLANE), dma(PLANE), dma(PLANE), dma(PLANE),
            dma(2, depth), dma(depth, PLANE), dma(depth, PLANE), dma(depth), dma(depth), dma(2),
        ],
        compiler_params=pltpu.CompilerParams(
            collective_id=0, has_side_effects=True, vmem_limit_bytes=62 * 2**20
        ),
        cost_estimate=pl.CostEstimate(
            flops=40 * 10**9, bytes_accessed=60 * 10**6, transcendentals=0
        ),
    )(patch, mlp_gain[None], up, down, kv_gain[None], kv_weight, byte_states, query_weight)


def attend_kernel(heads, distances, start, finish, scalars, ends, query, byte_patch, *refs):
    kv_refs, refs = refs[: len(distances)], refs[len(distances) :]
    if not start:
        (num_in, den_in), refs = refs[:2], refs[2:]
    if finish:
        out_weight, out, num, den = refs
    else:
        num, den = refs
    if start:
        num[...] = jnp.zeros_like(num)
        den[...] = jnp.zeros_like(den)
    else:
        num[...] = num_in[...]
        den[...] = den_in[...]
    tile = pl.program_id(0)
    lowest, highest = ends[2 * tile], ends[2 * tile + 1]
    scale = 2.0 / math.sqrt(HS) * math.log2(math.e)
    for distance, kv_ref in zip(distances, kv_refs):
        first, live = scalars[2 * distance], scalars[2 * distance + 1]
        for low in range(0, kv_ref.shape[0], KEY_TILE):
            last = first + jnp.minimum(live, low + KEY_TILE) - 1
            seen = (low < live) & (first + low <= highest) & (last > lowest - WIN)

            @pl.when(seen)
            def _(kv_ref=kv_ref, low=low, first=first, live=live):
                rows = query.shape[0]
                position = low + lax.broadcasted_iota(jnp.int32, (rows, KEY_TILE), 1)
                gap = byte_patch[...] - first - position
                usable = (position < live) & (gap >= 0) & (gap < WIN)
                for head in range(heads):
                    columns = slice(head * HS, (head + 1) * HS)
                    key = kv_ref[low : low + KEY_TILE, head * 2 * HS : head * 2 * HS + HS]
                    value = kv_ref[low : low + KEY_TILE, head * 2 * HS + HS : (head + 1) * 2 * HS]
                    scores = lax.dot_general(
                        query[:, columns],
                        key,
                        (((1,), (1,)), ((), ())),
                        preferred_element_type=jnp.float32,
                    )
                    weights = jnp.where(usable, jnp.exp2(scores * scale), 0.0)
                    den[:, columns] += weights[:, :HS] + weights[:, HS:]
                    num[:, columns] += jnp.dot(
                        weights.astype(jnp.bfloat16), value, preferred_element_type=jnp.float32
                    )

    if finish:
        parts = []
        for head in range(heads):
            columns = slice(head * HS, (head + 1) * HS)
            total = jnp.sum(den[:, columns], axis=1, keepdims=True)
            parts.append((num[:, columns] / total).astype(jnp.bfloat16))
        attended = jnp.concatenate(parts, axis=1)
        out[...] = jnp.dot(
            attended, out_weight[...], preferred_element_type=jnp.float32
        ).astype(jnp.bfloat16)


def attend(distances, scalars, ends, query, byte_patch, blocks, sums=None, out_weight=None):
    rows, width = query.shape
    heads = width // HS
    tile = rows // (ends.shape[0] // 2)
    start, finish = sums is None, out_weight is not None
    smem = pl.BlockSpec(memory_space=pltpu.SMEM)
    tiled = lambda columns: pl.BlockSpec((tile, columns), lambda i: (i, 0))
    whole = lambda array: pl.BlockSpec(array.shape, lambda i: (0, 0))
    operands = [scalars, ends, query, byte_patch, *blocks]
    in_specs = [smem, smem, tiled(width), tiled(1)] + [whole(block) for block in blocks]
    if not start:
        operands += list(sums)
        in_specs += [tiled(width), tiled(width)]
    if finish:
        operands.append(out_weight)
        in_specs.append(whole(out_weight))
        out_shape = jax.ShapeDtypeStruct((rows, out_weight.shape[1]), jnp.bfloat16)
        out_specs = tiled(out_weight.shape[1])
        scratch = [pltpu.VMEM((tile, width), jnp.float32)] * 2
    else:
        out_shape = [jax.ShapeDtypeStruct((rows, width), jnp.float32)] * 2
        out_specs = [tiled(width)] * 2
        scratch = []
    keys = sum(block.shape[0] for block in blocks)
    return pl.pallas_call(
        functools.partial(attend_kernel, heads, distances, start, finish),
        grid=(rows // tile,),
        in_specs=in_specs,
        out_specs=out_specs,
        out_shape=out_shape,
        scratch_shapes=scratch,
        compiler_params=pltpu.CompilerParams(vmem_limit_bytes=48 * 2**20),
        cost_estimate=pl.CostEstimate(
            flops=8 * rows * keys * width, bytes_accessed=4 * keys * width, transcendentals=0
        ),
    )(*operands)


def patch_block_plain(
    patch_states, mlp_gain, up_weight, down_weight, kv_gain, kv_weight, byte_states, query_weight
):
    seq = lax.axis_size("seq")
    patch_rows = patch_states.shape[0]
    size = PLANE if seq % PLANE == 0 else 1
    groups = [[base + i for i in range(size)] for base in range(0, seq, size)]
    across = [[base + i for base in range(0, seq, size)] for i in range(size)]
    place = lax.rem(lax.axis_index("seq"), size)

    up_part = lax.all_to_all(up_weight, "seq", 1, 0, axis_index_groups=groups, tiled=True)
    down_part = lax.all_to_all(down_weight, "seq", 0, 1, axis_index_groups=groups, tiled=True)
    up_all = lax.all_gather(up_part, "seq", axis=0, tiled=True, axis_index_groups=across)
    down_all = lax.all_gather(down_part, "seq", axis=1, tiled=True, axis_index_groups=across)

    normed = scale_rows(patch_states.astype(jnp.float32), mlp_gain.astype(jnp.float32)).astype(
        jnp.bfloat16
    )
    tokens = lax.all_gather(normed, "seq", axis=0, tiled=True, axis_index_groups=groups)
    heads_here = kv_weight.shape[1] // (2 * HS)
    bytes_here = byte_states.shape[0]
    query_proj = jnp.dot(byte_states, query_weight, preferred_element_type=jnp.float32).reshape(
        bytes_here, heads_here, HS
    )
    queries = unit_rows(query_proj).astype(jnp.bfloat16).reshape(bytes_here, heads_here * HS)

    preact = jnp.dot(tokens, up_all, preferred_element_type=jnp.float32)
    hidden = jax.nn.gelu(preact, approximate=False).astype(jnp.bfloat16)
    partial_value = jnp.dot(hidden, down_all, preferred_element_type=jnp.float32).astype(
        jnp.bfloat16
    )
    part = sum_over_cores(partial_value, 1).astype(jnp.bfloat16)
    part = part.reshape(size, patch_rows, part.shape[1])
    mixed = lax.dynamic_index_in_dim(part, place, 0, keepdims=False).astype(jnp.float32)
    for turn in range(1, size):
        pairs = [(base + i, base + (i ^ turn)) for base in range(0, seq, size) for i in range(size)]
        piece = lax.dynamic_index_in_dim(part, lax.bitwise_xor(place, turn), 0, keepdims=False)
        mixed = mixed + lax.ppermute(piece, "seq", pairs).astype(jnp.float32)
    mixed = join_cores(mixed.astype(jnp.bfloat16), 1).astype(jnp.float32)

    kv_in = scale_rows(
        patch_states.astype(jnp.float32) + mixed, kv_gain.astype(jnp.float32)
    ).astype(jnp.bfloat16)
    projected = jnp.dot(kv_in, kv_weight, preferred_element_type=jnp.float32).reshape(
        patch_rows, heads_here, 2, HS
    )
    kv_pack = (
        jnp.stack([unit_rows(projected[:, :, 0]), projected[:, :, 1]], axis=2)
        .astype(jnp.bfloat16)
        .reshape(patch_rows, heads_here * 2 * HS)
    )
    return kv_pack, queries


def on_device(
    patch_states,
    mlp_gain,
    up_weight,
    down_weight,
    kv_gain,
    kv_weight,
    byte_states,
    query_weight,
    out_weight,
    patch_counts,
    byte_patch,
):
    seq = lax.axis_size("seq")
    me = lax.axis_index("seq")
    patch_rows, features = patch_states.shape
    bytes_here = byte_states.shape[0]
    operands = (
        patch_states, mlp_gain, up_weight, down_weight, kv_gain, kv_weight, byte_states,
        query_weight,
    )
    fits = seq == 4 * PLANE and lax.axis_size("mp") == 2 and up_weight.shape[0] % 128 == 0
    if fits and up_weight.shape[1] % (PLANE * 128) == 0:
        kv_pack, queries = patch_block(*operands, seq // PLANE)
    else:
        kv_pack, queries = patch_block_plain(*operands)

    fewest = patch_rows // 2
    depth = (WIN + fewest - 2) // fewest
    own_count = patch_counts[0]
    blocks = [kv_pack]
    scalars = [jnp.zeros((), jnp.int32), own_count]
    first = jnp.zeros((), jnp.int32)
    for back in range(1, depth + 1):
        need = min(patch_rows, -(-(WIN - 1 - (back - 1) * fewest) // KEY_TILE) * KEY_TILE)
        source = kv_pack
        if need <= fewest:
            source = lax.dynamic_slice_in_dim(kv_pack, own_count - need, need, 0)
        blocks.append(
            lax.ppermute(source, "seq", [(i, i + back) for i in range(max(0, seq - back))])
        )
        held = lax.ppermute(own_count, "seq", [(i, i + back) for i in range(max(0, seq - back))])
        first = first - held
        if need <= fewest:
            scalars += [first + held - need, jnp.where(me >= back, need, 0)]
        else:
            scalars += [first, held]
    scalars = jnp.stack(scalars).astype(jnp.int32)
    tile = min(256, bytes_here)
    by_tile = byte_patch.reshape(bytes_here // tile, tile)
    ends = jnp.stack([by_tile[:, 0], by_tile[:, -1]], axis=1).reshape(-1)
    columns = byte_patch[:, None]
    sums = attend((0,), scalars, ends, queries, columns, blocks[:1])
    for back in range(1, depth):
        sums = attend((back,), scalars, ends, queries, columns, blocks[back : back + 1], sums)
    term = attend((depth,), scalars, ends, queries, columns, blocks[depth:], sums, out_weight)
    return sum_over_cores(term, 0).astype(jnp.bfloat16)


def solution(mesh):
    in_specs = (
        P("seq", None),
        P(),
        P("seq", "mp"),
        P("mp", "seq"),
        P(),
        P(None, "mp"),
        P("seq", None),
        P(None, "mp"),
        P("mp", None),
        P("seq"),
        P("seq"),
    )
    out_specs = P(("seq", "mp"), None)
    return jax.shard_map(
        on_device, mesh=mesh, in_specs=in_specs, out_specs=out_specs, check_vma=False
    )
```

```python
import functools
import math

import jax
import jax.numpy as jnp
from jax import lax
from jax.experimental import pallas as pl
from jax.experimental.pallas import tpu as pltpu
from jax.sharding import PartitionSpec as P

HS = 128
WIN = 1024
KEY_TILE = 256
PLANE = 4
TILE = 128


def scale_rows(values, gain):
    return values * lax.rsqrt(jnp.mean(values * values, axis=-1, keepdims=True) + 1e-05) * gain


def unit_rows(values):
    return values * lax.rsqrt(jnp.mean(values * values, axis=-1, keepdims=True) + 1e-06)


def sum_over_cores(value, scatter_dim):
    count = lax.axis_size("mp")
    if count != 2:
        return lax.psum_scatter(value, "mp", scatter_dimension=scatter_dim, tiled=True).astype(
            jnp.float32
        )
    me = lax.axis_index("mp")
    width = value.shape[scatter_dim] // 2
    theirs = lax.dynamic_slice_in_dim(value, (1 - me) * width, width, scatter_dim)
    mine = lax.dynamic_slice_in_dim(value, me * width, width, scatter_dim)
    got = lax.ppermute(theirs, "mp", [(0, 1), (1, 0)])
    return mine.astype(jnp.float32) + got.astype(jnp.float32)


def join_cores(value, dim):
    count = lax.axis_size("mp")
    if count != 2:
        return lax.all_gather(value, "mp", axis=dim, tiled=True)
    me = lax.axis_index("mp")
    got = lax.ppermute(value, "mp", [(0, 1), (1, 0)])
    first = jnp.where(me == 0, value, got)
    second = jnp.where(me == 0, got, value)
    return jnp.concatenate([first, second], axis=dim)


def block_kernel(
    patch, mlp_gain, up, down, kv_gain, kv_weight, byte_states, query_weight, count,
    kv_out, query_out, count_out,
    up_all, down_all, tokens, hidden, core_send, core_got, kept, plane_send, plane_got, mixed,
    swap_send, swap_recv, chunk_recv, right_send, left_send,
    token_send, token_recv, half_send, half_recv,
    core_sems, plane_sems, plane_recv, mixed_send, mixed_recv, local_sems,
    halo_send, halo_recv, count_send, count_recv,
):
    seq, core = lax.axis_index("seq"), lax.axis_index("mp")
    depth = lax.axis_size("seq") // PLANE
    z, place = seq // PLANE, lax.rem(seq, PLANE)
    y, x = place // 2, lax.rem(place, 2)
    rows, features = patch.shape
    thin = up.shape[0]
    units = up_all.shape[1]
    half = features // 2
    wide = features // (2 * depth)
    MESH = pl.DeviceIdType.MESH

    def member(turn):
        return 2 * lax.rem(y + turn // 2, 2) + lax.rem(x + lax.rem(turn, 2), 2)

    def peer(turn):
        return (z * PLANE + member(turn), core)

    partner = (seq, 1 - core)

    barrier = pltpu.get_barrier_semaphore()
    for turn in range(1, PLANE):
        pl.semaphore_signal(barrier, inc=1, device_id=peer(turn), device_id_type=MESH)
    pl.semaphore_signal(barrier, inc=1, device_id=partner, device_id_type=MESH)

    @pl.when(z > 0)
    def _():
        pl.semaphore_signal(barrier, inc=1, device_id=(seq - PLANE, core), device_id_type=MESH)

    @pl.when(z < depth - 1)
    def _():
        pl.semaphore_signal(barrier, inc=1, device_id=(seq + PLANE, core), device_id_type=MESH)

    pl.semaphore_wait(
        barrier, PLANE + jnp.where(z > 0, 1, 0) + jnp.where(z < depth - 1, 1, 0)
    )

    def remote(src, dst, send, recv, device):
        return pltpu.make_async_remote_copy(
            src_ref=src, dst_ref=dst, send_sem=send, recv_sem=recv, device_id=device,
            device_id_type=MESH,
        )

    def chunk(kind, index):
        if kind == 0:
            return up_all.at[pl.ds(pl.multiple_of(index * thin, thin), thin), :]
        return down_all.at[index]

    def held(kind, owner):
        start = pl.multiple_of(owner * units, units)
        if kind == 0:
            return up.at[:, pl.ds(start, units)]
        return down.at[pl.ds(start, units), :]

    def swap(kind, turn):
        index = z * PLANE + place
        return remote(
            held(kind, member(turn)), chunk(kind, index), swap_send.at[kind, turn],
            swap_recv.at[kind, turn], peer(turn),
        )

    def swap_arrives(kind, turn):
        index = z * PLANE + member(turn)
        return remote(
            chunk(kind, index), chunk(kind, index), swap_send.at[kind, turn],
            swap_recv.at[kind, turn], peer(turn),
        )

    def pass_right(kind, index):
        return remote(
            chunk(kind, index), chunk(kind, index), right_send.at[kind, index],
            chunk_recv.at[kind, index], (seq + PLANE, core),
        )

    def pass_left(kind, index):
        return remote(
            chunk(kind, index), chunk(kind, index), left_send.at[kind, index],
            chunk_recv.at[kind, index], (seq - PLANE, core),
        )

    def spread(kind, index):
        @pl.when(z < depth - 1)
        def _():
            pass_right(kind, index).start()

        @pl.when(z > 0)
        def _():
            pass_left(kind, index).start()

    def hop(kind, step):
        far, turn = step // PLANE, lax.rem(step, PLANE)

        @pl.when(z - 1 - far >= 0)
        def _():
            index = (z - 1 - far) * PLANE + member(turn)
            pass_left(kind, index).wait_recv()

            @pl.when(z < depth - 1)
            def _():
                pass_right(kind, index).start()

        @pl.when(z + 1 + far < depth)
        def _():
            index = (z + 1 + far) * PLANE + member(turn)
            pass_right(kind, index).wait_recv()

            @pl.when(z > 0)
            def _():
                pass_left(kind, index).start()

    own = [
        pltpu.make_async_copy(held(kind, place), chunk(kind, seq), local_sems.at[kind])
        for kind in range(2)
    ]
    for kind in range(2):
        own[kind].start()
    for turn in range(1, PLANE):
        swap(0, turn).start()
    own[0].wait()
    spread(0, seq)

    def later(turn):
        return member(turn) > place

    def source(turn):
        return jnp.where(later(turn), 0, PLANE)

    def distance(turn):
        return lax.rem(member(turn) - place + PLANE, PLANE)

    def from_distance(turn):
        return lax.rem(place - member(turn) + PLANE, PLANE)

    def count_on():
        return remote(
            count_out.at[0], count_out.at[PLANE], count_send.at[0], count_recv.at[0],
            (seq + PLANE, core),
        )

    def count_over(turn):
        return remote(
            count_out.at[source(turn)], count_out.at[distance(turn)], count_send.at[turn],
            count_recv.at[turn], peer(turn),
        )

    def count_arrives(turn):
        part = count_out.at[from_distance(turn)]
        return remote(part, part, count_send.at[turn], count_recv.at[turn], peer(turn))

    def count_chain():
        @pl.when(z > 0)
        def _():
            count_on().wait_recv()

        for turn in range(1, PLANE):
            @pl.when(later(turn) | (z > 0))
            def _(turn=turn):
                count_over(turn).start()

    count_out[0] = count[...]

    @pl.when(z < depth - 1)
    def _():
        count_on().start()

    def piece(step):
        return pl.ds(pl.multiple_of(step * TILE, TILE), TILE)

    def halo_on(step):
        return remote(
            kv_out.at[0, piece(step), :], kv_out.at[PLANE, piece(step), :],
            halo_send.at[0, step], halo_recv.at[0, step], (seq + PLANE, core),
        )

    def halo_over(turn, step):
        return remote(
            kv_out.at[source(turn), piece(step), :], kv_out.at[distance(turn), piece(step), :],
            halo_send.at[turn, step], halo_recv.at[turn, step], peer(turn),
        )

    def halo_arrives(turn, step):
        part = kv_out.at[from_distance(turn), piece(step), :]
        return remote(part, part, halo_send.at[turn, step], halo_recv.at[turn, step], peer(turn))

    gain = mlp_gain[...].astype(jnp.float32)
    row_start = pl.multiple_of(place * rows, rows)

    @pl.loop(0, rows // TILE)
    def _(tile):
        low = pl.multiple_of(tile * TILE, TILE)
        values = patch[pl.ds(low, TILE), :].astype(jnp.float32)
        tokens[pl.ds(row_start + low, TILE), :] = scale_rows(values, gain).astype(jnp.bfloat16)

    for turn in range(1, PLANE):
        swap_arrives(0, turn).wait_recv()
        spread(0, z * PLANE + member(turn))
    for turn in range(1, PLANE):
        swap(1, turn).start()

    def token_part(owner, side):
        return tokens.at[
            pl.ds(pl.multiple_of(owner * rows, rows), rows),
            pl.ds(pl.multiple_of(side * half, half), half),
        ]

    def send_tokens(turn):
        return remote(
            token_part(place, core), token_part(place, core), token_send.at[turn],
            token_recv.at[turn], peer(turn),
        )

    def tokens_arrive(turn):
        part = token_part(member(turn), core)
        return remote(part, part, token_send.at[turn], token_recv.at[turn], peer(turn))

    def half_over(turn):
        part = token_part(member(turn), core)
        return remote(part, part, half_send.at[turn], half_recv.at[turn], partner)

    def half_arrives(turn):
        part = token_part(member(turn), 1 - core)
        return remote(part, part, half_send.at[turn], half_recv.at[turn], partner)

    for turn in range(1, PLANE):
        send_tokens(turn).start()

    heads = query_weight.shape[1] // HS
    query_rows = byte_states.shape[0] // PLANE

    @pl.loop(0, PLANE)
    def _(step):
        low = pl.multiple_of(step * query_rows, query_rows)
        product = jnp.dot(
            byte_states[pl.ds(low, query_rows), :], query_weight[...],
            preferred_element_type=jnp.float32,
        )
        for head in range(heads):
            columns = slice(head * HS, (head + 1) * HS)
            query_out[pl.ds(low, query_rows), columns] = unit_rows(product[:, columns]).astype(
                jnp.bfloat16
            )
        hop(0, step)

    count_chain()
    own[1].wait()
    spread(1, seq)
    for turn in range(1, PLANE):
        swap_arrives(1, turn).wait_recv()
        spread(1, z * PLANE + member(turn))

    @pl.loop(PLANE, 2 * PLANE)
    def _(step):
        hop(0, step)

    for turn in range(1, PLANE):
        tokens_arrive(turn).wait_recv()
        half_over(turn).start()

    @pl.loop(2 * PLANE, (depth - 1) * PLANE)
    def _(step):
        hop(0, step)

    for turn in range(1, PLANE):
        half_arrives(turn).wait_recv()

    tall = PLANE * rows // (2 * PLANE)

    @pl.loop(0, 2 * PLANE)
    def _(step):
        low = pl.multiple_of(step * tall, tall)
        preact = jnp.dot(
            tokens[pl.ds(low, tall), :], up_all[...], preferred_element_type=jnp.float32
        )
        gelu = 0.5 * preact * (1.0 + lax.erf(preact * math.sqrt(0.5)))
        hidden[pl.ds(low, tall), :] = gelu.astype(jnp.bfloat16)
        hop(1, step)

    near = jnp.minimum(z, depth - 1 - z)

    def order(turn):
        swapped = jnp.where((near == 1) & (turn < 2), 1 - turn, turn)
        return jnp.where(z < depth // 2, swapped, depth - 1 - swapped)

    def plane_out(turn, to):
        start = pl.multiple_of(member(to) * rows, rows)
        return remote(
            plane_send.at[turn, pl.ds(start, rows), :], plane_got.at[turn, to],
            plane_sems.at[turn, to], plane_recv.at[turn, to], peer(to),
        )

    def core_swap(turn):
        return remote(
            core_send, core_got.at[turn], core_sems.at[0, turn], core_sems.at[1, turn], partner
        )

    def product(turn, side, out):
        chunks = order(turn) * PLANE + side * (PLANE // 2)
        weight = jnp.concatenate([down_all[chunks + i] for i in range(PLANE // 2)], axis=1)

        @pl.loop(0, PLANE)
        def _(owner):
            low = pl.multiple_of(owner * rows, rows)
            out[pl.ds(low, rows), :] = jnp.dot(
                hidden[pl.ds(low, rows), :], weight, preferred_element_type=jnp.float32
            ).astype(jnp.bfloat16)

    def one_block(turn):
        product(turn, 1 - core, core_send)
        core_swap(turn).start()
        product(turn, core, kept)
        core_swap(turn).wait()

        @pl.loop(0, PLANE)
        def _(owner):
            low = pl.multiple_of(owner * rows, rows)
            total = kept[pl.ds(low, rows), :].astype(jnp.float32) + core_got[
                turn, pl.ds(low, rows), :
            ].astype(jnp.float32)
            plane_send[turn, pl.ds(low, rows), :] = total.astype(jnp.bfloat16)

        for to in range(1, PLANE):
            plane_out(turn, to).start()

    @pl.loop(0, depth - 1)
    def _(turn):
        one_block(turn)

    @pl.loop(2 * PLANE, (depth - 1) * PLANE)
    def _(step):
        hop(1, step)

    one_block(depth - 1)

    def mixed_over(turn, side):
        part = mixed.at[2 * order(turn) + side]
        return remote(part, part, mixed_send.at[turn], mixed_recv.at[turn], partner)

    @pl.loop(0, depth)
    def _(turn):
        total = plane_send[turn, pl.ds(row_start, rows), :].astype(jnp.float32)
        for to in range(1, PLANE):
            plane_out(turn, to).wait_recv()
            total = total + plane_got[turn, to].astype(jnp.float32)
        mixed[2 * order(turn) + core] = total.astype(jnp.bfloat16)
        mixed_over(turn, core).start()

    @pl.loop(0, depth)
    def _(turn):
        mixed_over(turn, 1 - core).wait_recv()

    later_gain = kv_gain[...].astype(jnp.float32)

    @pl.loop(0, rows // TILE)
    def _(tile):
        low = pl.multiple_of(tile * TILE, TILE)
        more = jnp.concatenate(
            [mixed[i, pl.ds(low, TILE), :] for i in range(2 * depth)], axis=1
        )
        values = patch[pl.ds(low, TILE), :].astype(jnp.float32) + more.astype(jnp.float32)
        kv_in = scale_rows(values, later_gain).astype(jnp.bfloat16)
        projected = jnp.dot(kv_in, kv_weight[...], preferred_element_type=jnp.float32)
        for head in range(heads):
            key = slice(head * 2 * HS, head * 2 * HS + HS)
            value = slice(head * 2 * HS + HS, (head + 1) * 2 * HS)
            kv_out[0, pl.ds(low, TILE), key] = unit_rows(projected[:, key]).astype(jnp.bfloat16)
            kv_out[0, pl.ds(low, TILE), value] = projected[:, value].astype(jnp.bfloat16)

        @pl.when(z < depth - 1)
        def _():
            halo_on(tile).start()

        for turn in range(1, PLANE):
            @pl.when(later(turn))
            def _(turn=turn):
                halo_over(turn, tile).start()

    @pl.when(z > 0)
    def _():
        @pl.loop(0, rows // TILE)
        def _(step):
            halo_on(step).wait_recv()
            for turn in range(1, PLANE):
                @pl.when(member(turn) < place)
                def _(turn=turn):
                    halo_over(turn, step).start()

    for turn in range(1, PLANE):
        @pl.when((member(turn) < place) | (z > 0))
        def _(turn=turn):
            count_arrives(turn).wait_recv()

            @pl.loop(0, rows // TILE)
            def _(step):
                halo_arrives(turn, step).wait_recv()

    for turn in range(1, PLANE):
        @pl.when(later(turn) | (z > 0))
        def _(turn=turn):
            count_over(turn).wait_send()

            @pl.loop(0, rows // TILE)
            def _(step):
                halo_over(turn, step).wait_send()

    @pl.when(z < depth - 1)
    def _():
        count_on().wait_send()

        @pl.loop(0, rows // TILE)
        def _(step):
            halo_on(step).wait_send()

    for turn in range(1, PLANE):
        for kind in range(2):
            swap(kind, turn).wait_send()
        send_tokens(turn).wait_send()
        half_over(turn).wait_send()

    @pl.loop(0, depth)
    def _(turn):
        for to in range(1, PLANE):
            plane_out(turn, to).wait_send()
        mixed_over(turn, core).wait_send()

    @pl.loop(0, depth * PLANE)
    def _(index):
        @pl.when((z < depth - 1) & (index // PLANE <= z))
        def _():
            for kind in range(2):
                pass_right(kind, index).wait_send()

        @pl.when((z > 0) & (index // PLANE >= z))
        def _():
            for kind in range(2):
                pass_left(kind, index).wait_send()


def patch_block(
    patch, mlp_gain, up, down, kv_gain, kv_weight, byte_states, query_weight, count, depth
):
    rows, features = patch.shape
    thin = up.shape[0]
    units = up.shape[1] // PLANE
    wide = features // (2 * depth)
    vmem = pl.BlockSpec(memory_space=pltpu.VMEM)
    bf16 = lambda *shape: pltpu.VMEM(shape, jnp.bfloat16)
    dma = lambda *shape: pltpu.SemaphoreType.DMA(shape)
    return pl.pallas_call(
        block_kernel,
        in_specs=[vmem] * 9,
        out_specs=[vmem] * 3,
        out_shape=[
            jax.ShapeDtypeStruct((PLANE + 1, rows, kv_weight.shape[1]), jnp.bfloat16),
            jax.ShapeDtypeStruct((byte_states.shape[0], query_weight.shape[1]), jnp.bfloat16),
            jax.ShapeDtypeStruct((PLANE + 1, 8, 128), jnp.int32),
        ],
        scratch_shapes=[
            bf16(features, units),
            bf16(depth * PLANE, units, thin),
            bf16(PLANE * rows, features),
            bf16(PLANE * rows, units),
            bf16(PLANE * rows, wide),
            bf16(depth, PLANE * rows, wide),
            bf16(PLANE * rows, wide),
            bf16(depth, PLANE * rows, wide),
            bf16(depth, PLANE, rows, wide),
            bf16(2 * depth, rows, wide),
            dma(2, PLANE), dma(2, PLANE), dma(2, depth * PLANE),
            dma(2, depth * PLANE), dma(2, depth * PLANE),
            dma(PLANE), dma(PLANE), dma(PLANE), dma(PLANE),
            dma(2, depth), dma(depth, PLANE), dma(depth, PLANE), dma(depth), dma(depth), dma(2),
            dma(PLANE, rows // TILE), dma(PLANE, rows // TILE), dma(PLANE), dma(PLANE),
        ],
        compiler_params=pltpu.CompilerParams(
            collective_id=0, has_side_effects=True, vmem_limit_bytes=62 * 2**20
        ),
        cost_estimate=pl.CostEstimate(
            flops=40 * 10**9, bytes_accessed=60 * 10**6, transcendentals=0
        ),
    )(
        patch, mlp_gain[None], up, down, kv_gain[None], kv_weight, byte_states, query_weight,
        jnp.broadcast_to(count, (8, 128)),
    )


def attend_kernel(
    heads, blocks, counts, by_byte, query, byte_patch, kv, out_weight, out, num, den
):
    num[...] = jnp.zeros_like(num)
    den[...] = jnp.zeros_like(den)
    me = lax.axis_index("seq")
    rows = query.shape[0]
    tile = pl.program_id(0)
    lowest, highest = by_byte[tile * rows], by_byte[tile * rows + rows - 1]
    scale = 2.0 / math.sqrt(HS) * math.log2(math.e)
    slots = kv.shape[0] // blocks
    first = jnp.int32(0)
    for back in range(blocks):
        live = jnp.where(me >= back, counts[back], 0)
        if back:
            first = first - live
        for low in range(0, slots, KEY_TILE):
            last = first + jnp.minimum(live, low + KEY_TILE) - 1
            seen = (low < live) & (first + low <= highest) & (last > lowest - WIN)

            @pl.when(seen)
            def _(start=back * slots + low, low=low, first=first, live=live):
                position = low + lax.broadcasted_iota(jnp.int32, (rows, KEY_TILE), 1)
                gap = byte_patch[...] - first - position
                usable = (position < live) & (gap >= 0) & (gap < WIN)
                keys = slice(start, start + KEY_TILE)
                for head in range(heads):
                    columns = slice(head * HS, (head + 1) * HS)
                    scores = lax.dot_general(
                        query[:, columns],
                        kv[keys, head * 2 * HS : head * 2 * HS + HS],
                        (((1,), (1,)), ((), ())),
                        preferred_element_type=jnp.float32,
                    )
                    weights = jnp.where(usable, jnp.exp2(scores * scale), 0.0)
                    den[:, columns] += weights[:, :HS] + weights[:, HS:]
                    num[:, columns] += jnp.dot(
                        weights.astype(jnp.bfloat16),
                        kv[keys, head * 2 * HS + HS : (head + 1) * 2 * HS],
                        preferred_element_type=jnp.float32,
                    )

    parts = []
    for head in range(heads):
        columns = slice(head * HS, (head + 1) * HS)
        total = jnp.sum(den[:, columns], axis=1, keepdims=True)
        parts.append((num[:, columns] / total).astype(jnp.bfloat16))
    out[...] = jnp.dot(
        jnp.concatenate(parts, axis=1), out_weight[...], preferred_element_type=jnp.float32
    ).astype(jnp.bfloat16)


def attend(query, byte_patch, counts, kv, out_weight):
    rows, width = query.shape
    tile = min(256, rows)
    blocks = counts.shape[0]
    smem = pl.BlockSpec(memory_space=pltpu.SMEM)
    tiled = lambda columns: pl.BlockSpec((tile, columns), lambda i: (i, 0))
    whole = lambda array: pl.BlockSpec(array.shape, lambda i: (0, 0))
    return pl.pallas_call(
        functools.partial(attend_kernel, width // HS, blocks),
        grid=(rows // tile,),
        in_specs=[smem, smem, tiled(width), tiled(1), whole(kv), whole(out_weight)],
        out_specs=tiled(out_weight.shape[1]),
        out_shape=jax.ShapeDtypeStruct((rows, out_weight.shape[1]), jnp.bfloat16),
        scratch_shapes=[pltpu.VMEM((tile, width), jnp.float32)] * 2,
        compiler_params=pltpu.CompilerParams(vmem_limit_bytes=48 * 2**20),
        cost_estimate=pl.CostEstimate(
            flops=4 * rows * kv.shape[0] * width, bytes_accessed=4 * kv.size, transcendentals=0
        ),
    )(counts, byte_patch, query, byte_patch[:, None], kv, out_weight)


def patch_block_plain(
    patch_states, mlp_gain, up_weight, down_weight, kv_gain, kv_weight, byte_states, query_weight
):
    seq = lax.axis_size("seq")
    patch_rows = patch_states.shape[0]
    size = PLANE if seq % PLANE == 0 else 1
    groups = [[base + i for i in range(size)] for base in range(0, seq, size)]
    across = [[base + i for base in range(0, seq, size)] for i in range(size)]
    place = lax.rem(lax.axis_index("seq"), size)

    up_part = lax.all_to_all(up_weight, "seq", 1, 0, axis_index_groups=groups, tiled=True)
    down_part = lax.all_to_all(down_weight, "seq", 0, 1, axis_index_groups=groups, tiled=True)
    up_all = lax.all_gather(up_part, "seq", axis=0, tiled=True, axis_index_groups=across)
    down_all = lax.all_gather(down_part, "seq", axis=1, tiled=True, axis_index_groups=across)

    normed = scale_rows(patch_states.astype(jnp.float32), mlp_gain.astype(jnp.float32)).astype(
        jnp.bfloat16
    )
    tokens = lax.all_gather(normed, "seq", axis=0, tiled=True, axis_index_groups=groups)
    heads_here = kv_weight.shape[1] // (2 * HS)
    bytes_here = byte_states.shape[0]
    query_proj = jnp.dot(byte_states, query_weight, preferred_element_type=jnp.float32).reshape(
        bytes_here, heads_here, HS
    )
    queries = unit_rows(query_proj).astype(jnp.bfloat16).reshape(bytes_here, heads_here * HS)

    preact = jnp.dot(tokens, up_all, preferred_element_type=jnp.float32)
    hidden = jax.nn.gelu(preact, approximate=False).astype(jnp.bfloat16)
    partial_value = jnp.dot(hidden, down_all, preferred_element_type=jnp.float32).astype(
        jnp.bfloat16
    )
    part = sum_over_cores(partial_value, 1).astype(jnp.bfloat16)
    part = part.reshape(size, patch_rows, part.shape[1])
    mixed = lax.dynamic_index_in_dim(part, place, 0, keepdims=False).astype(jnp.float32)
    for turn in range(1, size):
        pairs = [(base + i, base + (i ^ turn)) for base in range(0, seq, size) for i in range(size)]
        piece = lax.dynamic_index_in_dim(part, lax.bitwise_xor(place, turn), 0, keepdims=False)
        mixed = mixed + lax.ppermute(piece, "seq", pairs).astype(jnp.float32)
    mixed = join_cores(mixed.astype(jnp.bfloat16), 1).astype(jnp.float32)

    kv_in = scale_rows(
        patch_states.astype(jnp.float32) + mixed, kv_gain.astype(jnp.float32)
    ).astype(jnp.bfloat16)
    projected = jnp.dot(kv_in, kv_weight, preferred_element_type=jnp.float32).reshape(
        patch_rows, heads_here, 2, HS
    )
    kv_pack = (
        jnp.stack([unit_rows(projected[:, :, 0]), projected[:, :, 1]], axis=2)
        .astype(jnp.bfloat16)
        .reshape(patch_rows, heads_here * 2 * HS)
    )
    return kv_pack, queries


def on_device(
    patch_states,
    mlp_gain,
    up_weight,
    down_weight,
    kv_gain,
    kv_weight,
    byte_states,
    query_weight,
    out_weight,
    patch_counts,
    byte_patch,
):
    seq = lax.axis_size("seq")
    patch_rows = patch_states.shape[0]
    operands = (
        patch_states, mlp_gain, up_weight, down_weight, kv_gain, kv_weight, byte_states,
        query_weight,
    )
    fewest = patch_rows // 2
    depth = (WIN + fewest - 2) // fewest
    fits = seq == 4 * PLANE and lax.axis_size("mp") == 2 and depth == PLANE
    fits = fits and up_weight.shape[0] % 128 == 0 and up_weight.shape[1] % (PLANE * 128) == 0
    if fits:
        kv_all, queries, counts = patch_block(*operands, patch_counts, seq // PLANE)
        counts = counts[:, 0, 0]
    else:
        kv_pack, queries = patch_block_plain(*operands)
        kv_all, counts = [kv_pack], [patch_counts]
        for back in range(1, depth + 1):
            pairs = [(i, i + back) for i in range(max(0, seq - back))]
            kv_all.append(lax.ppermute(kv_pack, "seq", pairs))
            counts.append(lax.ppermute(patch_counts, "seq", pairs))
        kv_all, counts = jnp.stack(kv_all), jnp.concatenate(counts)
    kv_all = kv_all.reshape((depth + 1) * patch_rows, kv_all.shape[2])
    term = attend(queries, byte_patch, counts, kv_all, out_weight)
    return sum_over_cores(term, 0).astype(jnp.bfloat16)


def solution(mesh):
    in_specs = (
        P("seq", None),
        P(),
        P("seq", "mp"),
        P("mp", "seq"),
        P(),
        P(None, "mp"),
        P("seq", None),
        P(None, "mp"),
        P("mp", None),
        P("seq"),
        P("seq"),
    )
    out_specs = P(("seq", "mp"), None)
    return jax.shard_map(
        on_device, mesh=mesh, in_specs=in_specs, out_specs=out_specs, check_vma=False
    )
```

```python
import functools
import math

import jax
import jax.numpy as jnp
from jax import lax
from jax.experimental import pallas as pl
from jax.experimental.pallas import tpu as pltpu
from jax.sharding import PartitionSpec as P

HS = 128
WIN = 1024
KEY_TILE = 256
PLANE = 4
TILE = 128


def scale_rows(values, gain):
    return values * lax.rsqrt(jnp.mean(values * values, axis=-1, keepdims=True) + 1e-05) * gain


def unit_rows(values):
    return values * lax.rsqrt(jnp.mean(values * values, axis=-1, keepdims=True) + 1e-06)


def sum_over_cores(value, scatter_dim):
    count = lax.axis_size("mp")
    if count != 2:
        return lax.psum_scatter(value, "mp", scatter_dimension=scatter_dim, tiled=True).astype(
            jnp.float32
        )
    me = lax.axis_index("mp")
    width = value.shape[scatter_dim] // 2
    theirs = lax.dynamic_slice_in_dim(value, (1 - me) * width, width, scatter_dim)
    mine = lax.dynamic_slice_in_dim(value, me * width, width, scatter_dim)
    got = lax.ppermute(theirs, "mp", [(0, 1), (1, 0)])
    return mine.astype(jnp.float32) + got.astype(jnp.float32)


def join_cores(value, dim):
    count = lax.axis_size("mp")
    if count != 2:
        return lax.all_gather(value, "mp", axis=dim, tiled=True)
    me = lax.axis_index("mp")
    got = lax.ppermute(value, "mp", [(0, 1), (1, 0)])
    first = jnp.where(me == 0, value, got)
    second = jnp.where(me == 0, got, value)
    return jnp.concatenate([first, second], axis=dim)


def block_kernel(
    patch, mlp_gain, up, down, kv_gain, kv_weight, byte_states, query_weight, count,
    byte_patch, out_weight,
    out,
    kv_out, query_out, count_out, num, den, term_send, term_kept, term_got,
    up_all, down_all, tokens, hidden, core_send, core_got, kept, plane_send, plane_got, mixed,
    swap_send, swap_recv, chunk_recv, right_send, left_send,
    token_send, token_recv, half_send, half_recv,
    core_sems, plane_sems, plane_recv, mixed_send, mixed_recv, local_sems,
    halo_send, halo_recv, count_send, count_recv, term_sems, term_recv,
):
    seq, core = lax.axis_index("seq"), lax.axis_index("mp")
    depth = lax.axis_size("seq") // PLANE
    z, place = seq // PLANE, lax.rem(seq, PLANE)
    y, x = place // 2, lax.rem(place, 2)
    rows, features = patch.shape
    thin = up.shape[0]
    units = up_all.shape[1]
    half = features // 2
    wide = features // (2 * depth)
    MESH = pl.DeviceIdType.MESH

    def member(turn):
        return 2 * lax.rem(y + turn // 2, 2) + lax.rem(x + lax.rem(turn, 2), 2)

    def peer(turn):
        return (z * PLANE + member(turn), core)

    partner = (seq, 1 - core)

    barrier = pltpu.get_barrier_semaphore()
    for turn in range(1, PLANE):
        pl.semaphore_signal(barrier, inc=1, device_id=peer(turn), device_id_type=MESH)
    pl.semaphore_signal(barrier, inc=1, device_id=partner, device_id_type=MESH)

    @pl.when(z > 0)
    def _():
        pl.semaphore_signal(barrier, inc=1, device_id=(seq - PLANE, core), device_id_type=MESH)

    @pl.when(z < depth - 1)
    def _():
        pl.semaphore_signal(barrier, inc=1, device_id=(seq + PLANE, core), device_id_type=MESH)

    pl.semaphore_wait(
        barrier, PLANE + jnp.where(z > 0, 1, 0) + jnp.where(z < depth - 1, 1, 0)
    )

    def remote(src, dst, send, recv, device):
        return pltpu.make_async_remote_copy(
            src_ref=src, dst_ref=dst, send_sem=send, recv_sem=recv, device_id=device,
            device_id_type=MESH,
        )

    def chunk(kind, index):
        if kind == 0:
            return up_all.at[pl.ds(pl.multiple_of(index * thin, thin), thin), :]
        return down_all.at[index]

    def held(kind, owner):
        start = pl.multiple_of(owner * units, units)
        if kind == 0:
            return up.at[:, pl.ds(start, units)]
        return down.at[pl.ds(start, units), :]

    def swap(kind, turn):
        index = z * PLANE + place
        return remote(
            held(kind, member(turn)), chunk(kind, index), swap_send.at[kind, turn],
            swap_recv.at[kind, turn], peer(turn),
        )

    def swap_arrives(kind, turn):
        index = z * PLANE + member(turn)
        return remote(
            chunk(kind, index), chunk(kind, index), swap_send.at[kind, turn],
            swap_recv.at[kind, turn], peer(turn),
        )

    def pass_right(kind, index):
        return remote(
            chunk(kind, index), chunk(kind, index), right_send.at[kind, index],
            chunk_recv.at[kind, index], (seq + PLANE, core),
        )

    def pass_left(kind, index):
        return remote(
            chunk(kind, index), chunk(kind, index), left_send.at[kind, index],
            chunk_recv.at[kind, index], (seq - PLANE, core),
        )

    def spread(kind, index):
        @pl.when(z < depth - 1)
        def _():
            pass_right(kind, index).start()

        @pl.when(z > 0)
        def _():
            pass_left(kind, index).start()

    def hop(kind, step):
        far, turn = step // PLANE, lax.rem(step, PLANE)

        @pl.when(z - 1 - far >= 0)
        def _():
            index = (z - 1 - far) * PLANE + member(turn)
            pass_left(kind, index).wait_recv()

            @pl.when(z < depth - 1)
            def _():
                pass_right(kind, index).start()

        @pl.when(z + 1 + far < depth)
        def _():
            index = (z + 1 + far) * PLANE + member(turn)
            pass_right(kind, index).wait_recv()

            @pl.when(z > 0)
            def _():
                pass_left(kind, index).start()

    own = [
        pltpu.make_async_copy(held(kind, place), chunk(kind, seq), local_sems.at[kind])
        for kind in range(2)
    ]
    for kind in range(2):
        own[kind].start()
    for turn in range(1, PLANE):
        swap(0, turn).start()
    own[0].wait()
    spread(0, seq)

    def later(turn):
        return member(turn) > place

    def source(turn):
        return jnp.where(later(turn), 0, PLANE)

    def distance(turn):
        return lax.rem(member(turn) - place + PLANE, PLANE)

    def from_distance(turn):
        return lax.rem(place - member(turn) + PLANE, PLANE)

    def count_on():
        return remote(
            count_out.at[0], count_out.at[PLANE], count_send.at[0], count_recv.at[0],
            (seq + PLANE, core),
        )

    def count_over(turn):
        return remote(
            count_out.at[source(turn)], count_out.at[distance(turn)], count_send.at[turn],
            count_recv.at[turn], peer(turn),
        )

    def count_arrives(turn):
        part = count_out.at[from_distance(turn)]
        return remote(part, part, count_send.at[turn], count_recv.at[turn], peer(turn))

    def count_chain():
        @pl.when(z > 0)
        def _():
            count_on().wait_recv()

        for turn in range(1, PLANE):
            @pl.when(later(turn) | (z > 0))
            def _(turn=turn):
                count_over(turn).start()

    count_out[0] = count[...]
    num[...] = jnp.zeros_like(num)
    den[...] = jnp.zeros_like(den)

    @pl.when(z < depth - 1)
    def _():
        count_on().start()

    def piece(step):
        return pl.ds(pl.multiple_of(step * TILE, TILE), TILE)

    def halo_on(step):
        return remote(
            kv_out.at[0, piece(step), :], kv_out.at[PLANE, piece(step), :],
            halo_send.at[0, step], halo_recv.at[0, step], (seq + PLANE, core),
        )

    def halo_over(turn, step):
        return remote(
            kv_out.at[source(turn), piece(step), :], kv_out.at[distance(turn), piece(step), :],
            halo_send.at[turn, step], halo_recv.at[turn, step], peer(turn),
        )

    def halo_arrives(turn, step):
        part = kv_out.at[from_distance(turn), piece(step), :]
        return remote(part, part, halo_send.at[turn, step], halo_recv.at[turn, step], peer(turn))

    gain = mlp_gain[...].astype(jnp.float32)
    row_start = pl.multiple_of(place * rows, rows)

    @pl.loop(0, rows // TILE)
    def _(tile):
        low = pl.multiple_of(tile * TILE, TILE)
        values = patch[pl.ds(low, TILE), :].astype(jnp.float32)
        tokens[pl.ds(row_start + low, TILE), :] = scale_rows(values, gain).astype(jnp.bfloat16)

    for turn in range(1, PLANE):
        swap_arrives(0, turn).wait_recv()
        spread(0, z * PLANE + member(turn))
    for turn in range(1, PLANE):
        swap(1, turn).start()

    def token_part(owner, side):
        return tokens.at[
            pl.ds(pl.multiple_of(owner * rows, rows), rows),
            pl.ds(pl.multiple_of(side * half, half), half),
        ]

    def send_tokens(turn):
        return remote(
            token_part(place, core), token_part(place, core), token_send.at[turn],
            token_recv.at[turn], peer(turn),
        )

    def tokens_arrive(turn):
        part = token_part(member(turn), core)
        return remote(part, part, token_send.at[turn], token_recv.at[turn], peer(turn))

    def half_over(turn):
        part = token_part(member(turn), core)
        return remote(part, part, half_send.at[turn], half_recv.at[turn], partner)

    def half_arrives(turn):
        part = token_part(member(turn), 1 - core)
        return remote(part, part, half_send.at[turn], half_recv.at[turn], partner)

    for turn in range(1, PLANE):
        send_tokens(turn).start()

    heads = query_weight.shape[1] // HS
    query_rows = byte_states.shape[0] // PLANE

    @pl.loop(0, PLANE)
    def _(step):
        low = pl.multiple_of(step * query_rows, query_rows)
        product = jnp.dot(
            byte_states[pl.ds(low, query_rows), :], query_weight[...],
            preferred_element_type=jnp.float32,
        )
        for head in range(heads):
            columns = slice(head * HS, (head + 1) * HS)
            query_out[pl.ds(low, query_rows), columns] = unit_rows(product[:, columns]).astype(
                jnp.bfloat16
            )
        hop(0, step)

    count_chain()
    own[1].wait()
    spread(1, seq)
    for turn in range(1, PLANE):
        swap_arrives(1, turn).wait_recv()
        spread(1, z * PLANE + member(turn))

    @pl.loop(PLANE, 2 * PLANE)
    def _(step):
        hop(0, step)

    for turn in range(1, PLANE):
        tokens_arrive(turn).wait_recv()
        half_over(turn).start()

    @pl.loop(2 * PLANE, (depth - 1) * PLANE)
    def _(step):
        hop(0, step)

    for turn in range(1, PLANE):
        half_arrives(turn).wait_recv()

    tall = PLANE * rows // (2 * PLANE)

    @pl.loop(0, 2 * PLANE)
    def _(step):
        low = pl.multiple_of(step * tall, tall)
        preact = jnp.dot(
            tokens[pl.ds(low, tall), :], up_all[...], preferred_element_type=jnp.float32
        )
        gelu = 0.5 * preact * (1.0 + lax.erf(preact * math.sqrt(0.5)))
        hidden[pl.ds(low, tall), :] = gelu.astype(jnp.bfloat16)
        hop(1, step)

    for turn in range(1, PLANE):
        send_tokens(turn).wait_send()
        half_over(turn).wait_send()
    kv_held = tokens.at[:, 0:half]
    out_held = tokens.at[0 : out_weight.shape[0], half : 2 * half]
    kv_load = pltpu.make_async_copy(kv_weight, kv_held, local_sems.at[0])
    out_load = pltpu.make_async_copy(out_weight, out_held, local_sems.at[1])
    kv_load.start()
    out_load.start()

    near = jnp.minimum(z, depth - 1 - z)

    def order(turn):
        swapped = jnp.where((near == 1) & (turn < 2), 1 - turn, turn)
        return jnp.where(z < depth // 2, swapped, depth - 1 - swapped)

    def plane_out(turn, to):
        start = pl.multiple_of(member(to) * rows, rows)
        return remote(
            plane_send.at[turn, pl.ds(start, rows), :], plane_got.at[turn, to - 1],
            plane_sems.at[turn, to], plane_recv.at[turn, to], peer(to),
        )

    def core_swap(turn):
        return remote(
            core_send, core_got.at[turn], core_sems.at[0, turn], core_sems.at[1, turn], partner
        )

    def product(turn, side, out):
        chunks = order(turn) * PLANE + side * (PLANE // 2)
        weight = jnp.concatenate([down_all[chunks + i] for i in range(PLANE // 2)], axis=1)

        @pl.loop(0, PLANE)
        def _(owner):
            low = pl.multiple_of(owner * rows, rows)
            out[pl.ds(low, rows), :] = jnp.dot(
                hidden[pl.ds(low, rows), :], weight, preferred_element_type=jnp.float32
            ).astype(jnp.bfloat16)

    def one_block(turn):
        product(turn, 1 - core, core_send)
        core_swap(turn).start()
        product(turn, core, kept)
        core_swap(turn).wait()

        @pl.loop(0, PLANE)
        def _(owner):
            low = pl.multiple_of(owner * rows, rows)
            total = kept[pl.ds(low, rows), :].astype(jnp.float32) + core_got[
                turn, pl.ds(low, rows), :
            ].astype(jnp.float32)
            plane_send[turn, pl.ds(low, rows), :] = total.astype(jnp.bfloat16)

        for to in range(1, PLANE):
            plane_out(turn, to).start()

    @pl.loop(0, depth - 1)
    def _(turn):
        one_block(turn)

    @pl.loop(2 * PLANE, (depth - 1) * PLANE)
    def _(step):
        hop(1, step)

    one_block(depth - 1)

    def mixed_over(turn, side):
        part = mixed.at[2 * order(turn) + side]
        return remote(part, part, mixed_send.at[turn], mixed_recv.at[turn], partner)

    @pl.loop(0, depth)
    def _(turn):
        total = plane_send[turn, pl.ds(row_start, rows), :].astype(jnp.float32)
        for to in range(1, PLANE):
            plane_out(turn, to).wait_recv()
            total = total + plane_got[turn, to - 1].astype(jnp.float32)
        mixed[2 * order(turn) + core] = total.astype(jnp.bfloat16)
        mixed_over(turn, core).start()

    @pl.loop(0, depth)
    def _(turn):
        mixed_over(turn, 1 - core).wait_recv()

    kv_load.wait()
    out_load.wait()
    later_gain = kv_gain[...].astype(jnp.float32)

    @pl.loop(0, rows // TILE)
    def _(tile):
        low = pl.multiple_of(tile * TILE, TILE)
        more = jnp.concatenate(
            [mixed[i, pl.ds(low, TILE), :] for i in range(2 * depth)], axis=1
        )
        values = patch[pl.ds(low, TILE), :].astype(jnp.float32) + more.astype(jnp.float32)
        kv_in = scale_rows(values, later_gain).astype(jnp.bfloat16)
        projected = jnp.dot(kv_in, kv_held[...], preferred_element_type=jnp.float32)
        for head in range(heads):
            key = slice(head * 2 * HS, head * 2 * HS + HS)
            value = slice(head * 2 * HS + HS, (head + 1) * 2 * HS)
            kv_out[0, pl.ds(low, TILE), key] = unit_rows(projected[:, key]).astype(jnp.bfloat16)
            kv_out[0, pl.ds(low, TILE), value] = projected[:, value].astype(jnp.bfloat16)

        @pl.when(z < depth - 1)
        def _():
            halo_on(tile).start()

        for turn in range(1, PLANE - 1):
            @pl.when(later(turn))
            def _(turn=turn):
                halo_over(turn, tile).start()

    @pl.when(later(PLANE - 1))
    def _():
        @pl.loop(0, rows // TILE)
        def _(step):
            halo_over(PLANE - 1, step).start()

    scale = 2.0 / math.sqrt(HS) * math.log2(math.e)
    byte_rows = byte_patch.shape[0] // PLANE

    def attend_tile(slot, tile):
        low = pl.multiple_of(tile * byte_rows, byte_rows)
        here = pl.ds(low, byte_rows)
        live = count_out[slot][0:1, 0:1]
        before = jnp.zeros((1, 1), jnp.int32)
        for back in range(1, PLANE + 1):
            before = before + jnp.where(slot >= back, count_out[back][0:1, 0:1], 0)
        mine = byte_patch[here, :] + before
        for start in range(0, rows, KEY_TILE):
            position = start + lax.broadcasted_iota(jnp.int32, (byte_rows, KEY_TILE), 1)
            gap = mine - position
            usable = (position < live) & (gap >= 0) & (gap < WIN)
            keys = slice(start, start + KEY_TILE)
            scores = [
                lax.dot_general(
                    query_out[here, head * HS : (head + 1) * HS],
                    kv_out[slot, keys, head * 2 * HS : head * 2 * HS + HS],
                    (((1,), (1,)), ((), ())),
                    preferred_element_type=jnp.float32,
                )
                for head in range(heads)
            ]
            weights = [jnp.where(usable, jnp.exp2(score * scale), 0.0) for score in scores]
            for head in range(heads):
                columns = slice(head * HS, (head + 1) * HS)
                weight = weights[head]
                den[here, columns] += weight[:, :HS] + weight[:, HS:]
                num[here, columns] += jnp.dot(
                    weight.astype(jnp.bfloat16),
                    kv_out[slot, keys, head * 2 * HS + HS : (head + 1) * 2 * HS],
                    preferred_element_type=jnp.float32,
                )

    @pl.loop(0, PLANE)
    def _(step):
        @pl.when(z > 0)
        def _():
            halo_on(step).wait_recv()
            for turn in range(1, PLANE - 1):
                @pl.when(member(turn) < place)
                def _(turn=turn):
                    halo_over(turn, step).start()

        attend_tile(0, step)

    @pl.when((z > 0) & (member(PLANE - 1) < place))
    def _():
        @pl.loop(0, rows // TILE)
        def _(step):
            halo_over(PLANE - 1, step).start()

    for turn in range(1, PLANE):
        @pl.when((member(turn) < place) | (z > 0))
        def _(turn=turn):
            count_arrives(turn).wait_recv()

    @pl.when(z > 0)
    def _():
        @pl.loop(0, PLANE)
        def _(tile):
            attend_tile(PLANE, tile)

    @pl.loop(1, PLANE)
    def _(turn):
        @pl.when((member(turn) < place) | (z > 0))
        def _():
            @pl.loop(0, rows // TILE)
            def _(step):
                halo_arrives(turn, step).wait_recv()

            @pl.loop(0, PLANE)
            def _(tile):
                attend_tile(from_distance(turn), tile)

    def finish(tile):
        low = pl.multiple_of(tile * byte_rows, byte_rows)
        parts = []
        for head in range(heads):
            columns = slice(head * HS, (head + 1) * HS)
            total = jnp.sum(den[pl.ds(low, byte_rows), columns], axis=1, keepdims=True)
            parts.append((num[pl.ds(low, byte_rows), columns] / total).astype(jnp.bfloat16))
        return jnp.dot(
            jnp.concatenate(parts, axis=1), out_held[...], preferred_element_type=jnp.float32
        ).astype(jnp.bfloat16)

    pair = PLANE // 2

    def term_over(tile):
        return remote(
            term_send.at[tile], term_got.at[tile], term_sems.at[tile], term_recv.at[tile], partner
        )

    @pl.loop(0, pair)
    def _(tile):
        term_send[tile] = finish((1 - core) * pair + tile)
        term_over(tile).start()

    @pl.loop(0, pair)
    def _(tile):
        term_kept[tile] = finish(core * pair + tile)

    @pl.loop(0, pair)
    def _(tile):
        term_over(tile).wait()
        total = term_kept[tile].astype(jnp.float32) + term_got[tile].astype(jnp.float32)
        out[pl.ds(pl.multiple_of(tile * byte_rows, byte_rows), byte_rows), :] = total.astype(
            jnp.bfloat16
        )

    for turn in range(1, PLANE):
        @pl.when(later(turn) | (z > 0))
        def _(turn=turn):
            count_over(turn).wait_send()

            @pl.loop(0, rows // TILE)
            def _(step):
                halo_over(turn, step).wait_send()

    @pl.when(z < depth - 1)
    def _():
        count_on().wait_send()

        @pl.loop(0, rows // TILE)
        def _(step):
            halo_on(step).wait_send()

    for turn in range(1, PLANE):
        for kind in range(2):
            swap(kind, turn).wait_send()

    @pl.loop(0, depth)
    def _(turn):
        for to in range(1, PLANE):
            plane_out(turn, to).wait_send()
        mixed_over(turn, core).wait_send()

    @pl.loop(0, depth * PLANE)
    def _(index):
        @pl.when((z < depth - 1) & (index // PLANE <= z))
        def _():
            for kind in range(2):
                pass_right(kind, index).wait_send()

        @pl.when((z > 0) & (index // PLANE >= z))
        def _():
            for kind in range(2):
                pass_left(kind, index).wait_send()


def patch_block(
    patch, mlp_gain, up, down, kv_gain, kv_weight, byte_states, query_weight, count,
    byte_patch, out_weight, depth
):
    rows, features = patch.shape
    thin = up.shape[0]
    units = up.shape[1] // PLANE
    wide = features // (2 * depth)
    bytes_here, width = byte_states.shape[0], out_weight.shape[1]
    vmem = pl.BlockSpec(memory_space=pltpu.VMEM)
    hbm = pl.BlockSpec(memory_space=pl.ANY)
    bf16 = lambda *shape: pltpu.VMEM(shape, jnp.bfloat16)
    dma = lambda *shape: pltpu.SemaphoreType.DMA(shape)
    return pl.pallas_call(
        block_kernel,
        in_specs=[vmem] * 5 + [hbm] + [vmem] * 4 + [hbm],
        out_specs=vmem,
        out_shape=jax.ShapeDtypeStruct((bytes_here // 2, width), jnp.bfloat16),
        scratch_shapes=[
            bf16(PLANE + 1, rows, kv_weight.shape[1]),
            bf16(bytes_here, query_weight.shape[1]),
            pltpu.VMEM((PLANE + 1, 8, 128), jnp.int32),
            pltpu.VMEM((bytes_here, query_weight.shape[1]), jnp.float32),
            pltpu.VMEM((bytes_here, query_weight.shape[1]), jnp.float32),
            bf16(2, bytes_here // 4, width),
            bf16(2, bytes_here // 4, width),
            bf16(2, bytes_here // 4, width),
            bf16(features, units),
            bf16(depth * PLANE, units, thin),
            bf16(PLANE * rows, features),
            bf16(PLANE * rows, units),
            bf16(PLANE * rows, wide),
            bf16(depth, PLANE * rows, wide),
            bf16(PLANE * rows, wide),
            bf16(depth, PLANE * rows, wide),
            bf16(depth, PLANE - 1, rows, wide),
            bf16(2 * depth, rows, wide),
            dma(2, PLANE), dma(2, PLANE), dma(2, depth * PLANE),
            dma(2, depth * PLANE), dma(2, depth * PLANE),
            dma(PLANE), dma(PLANE), dma(PLANE), dma(PLANE),
            dma(2, depth), dma(depth, PLANE), dma(depth, PLANE), dma(depth), dma(depth), dma(2),
            dma(PLANE, rows // TILE), dma(PLANE, rows // TILE), dma(PLANE), dma(PLANE),
            dma(2), dma(2),
        ],
        compiler_params=pltpu.CompilerParams(
            collective_id=0, has_side_effects=True, vmem_limit_bytes=60 * 2**20
        ),
        cost_estimate=pl.CostEstimate(
            flops=40 * 10**9, bytes_accessed=60 * 10**6, transcendentals=0
        ),
    )(
        patch, mlp_gain[None], up, down, kv_gain[None], kv_weight, byte_states, query_weight,
        jnp.broadcast_to(count, (8, 128)), byte_patch[:, None], out_weight,
    )


def attend_kernel(
    heads, blocks, counts, by_byte, query, byte_patch, kv, out_weight, out, num, den
):
    num[...] = jnp.zeros_like(num)
    den[...] = jnp.zeros_like(den)
    me = lax.axis_index("seq")
    rows = query.shape[0]
    tile = pl.program_id(0)
    lowest, highest = by_byte[tile * rows], by_byte[tile * rows + rows - 1]
    scale = 2.0 / math.sqrt(HS) * math.log2(math.e)
    slots = kv.shape[0] // blocks
    first = jnp.int32(0)
    for back in range(blocks):
        live = jnp.where(me >= back, counts[back], 0)
        if back:
            first = first - live
        for low in range(0, slots, KEY_TILE):
            last = first + jnp.minimum(live, low + KEY_TILE) - 1
            seen = (low < live) & (first + low <= highest) & (last > lowest - WIN)

            @pl.when(seen)
            def _(start=back * slots + low, low=low, first=first, live=live):
                position = low + lax.broadcasted_iota(jnp.int32, (rows, KEY_TILE), 1)
                gap = byte_patch[...] - first - position
                usable = (position < live) & (gap >= 0) & (gap < WIN)
                keys = slice(start, start + KEY_TILE)
                for head in range(heads):
                    columns = slice(head * HS, (head + 1) * HS)
                    scores = lax.dot_general(
                        query[:, columns],
                        kv[keys, head * 2 * HS : head * 2 * HS + HS],
                        (((1,), (1,)), ((), ())),
                        preferred_element_type=jnp.float32,
                    )
                    weights = jnp.where(usable, jnp.exp2(scores * scale), 0.0)
                    den[:, columns] += weights[:, :HS] + weights[:, HS:]
                    num[:, columns] += jnp.dot(
                        weights.astype(jnp.bfloat16),
                        kv[keys, head * 2 * HS + HS : (head + 1) * 2 * HS],
                        preferred_element_type=jnp.float32,
                    )

    parts = []
    for head in range(heads):
        columns = slice(head * HS, (head + 1) * HS)
        total = jnp.sum(den[:, columns], axis=1, keepdims=True)
        parts.append((num[:, columns] / total).astype(jnp.bfloat16))
    out[...] = jnp.dot(
        jnp.concatenate(parts, axis=1), out_weight[...], preferred_element_type=jnp.float32
    ).astype(jnp.bfloat16)


def attend(query, byte_patch, counts, kv, out_weight):
    rows, width = query.shape
    tile = min(256, rows)
    blocks = counts.shape[0]
    smem = pl.BlockSpec(memory_space=pltpu.SMEM)
    tiled = lambda columns: pl.BlockSpec((tile, columns), lambda i: (i, 0))
    whole = lambda array: pl.BlockSpec(array.shape, lambda i: (0, 0))
    return pl.pallas_call(
        functools.partial(attend_kernel, width // HS, blocks),
        grid=(rows // tile,),
        in_specs=[smem, smem, tiled(width), tiled(1), whole(kv), whole(out_weight)],
        out_specs=tiled(out_weight.shape[1]),
        out_shape=jax.ShapeDtypeStruct((rows, out_weight.shape[1]), jnp.bfloat16),
        scratch_shapes=[pltpu.VMEM((tile, width), jnp.float32)] * 2,
        compiler_params=pltpu.CompilerParams(vmem_limit_bytes=48 * 2**20),
        cost_estimate=pl.CostEstimate(
            flops=4 * rows * kv.shape[0] * width, bytes_accessed=4 * kv.size, transcendentals=0
        ),
    )(counts, byte_patch, query, byte_patch[:, None], kv, out_weight)


def patch_block_plain(
    patch_states, mlp_gain, up_weight, down_weight, kv_gain, kv_weight, byte_states, query_weight
):
    seq = lax.axis_size("seq")
    patch_rows = patch_states.shape[0]
    size = PLANE if seq % PLANE == 0 else 1
    groups = [[base + i for i in range(size)] for base in range(0, seq, size)]
    across = [[base + i for base in range(0, seq, size)] for i in range(size)]
    place = lax.rem(lax.axis_index("seq"), size)

    up_part = lax.all_to_all(up_weight, "seq", 1, 0, axis_index_groups=groups, tiled=True)
    down_part = lax.all_to_all(down_weight, "seq", 0, 1, axis_index_groups=groups, tiled=True)
    up_all = lax.all_gather(up_part, "seq", axis=0, tiled=True, axis_index_groups=across)
    down_all = lax.all_gather(down_part, "seq", axis=1, tiled=True, axis_index_groups=across)

    normed = scale_rows(patch_states.astype(jnp.float32), mlp_gain.astype(jnp.float32)).astype(
        jnp.bfloat16
    )
    tokens = lax.all_gather(normed, "seq", axis=0, tiled=True, axis_index_groups=groups)
    heads_here = kv_weight.shape[1] // (2 * HS)
    bytes_here = byte_states.shape[0]
    query_proj = jnp.dot(byte_states, query_weight, preferred_element_type=jnp.float32).reshape(
        bytes_here, heads_here, HS
    )
    queries = unit_rows(query_proj).astype(jnp.bfloat16).reshape(bytes_here, heads_here * HS)

    preact = jnp.dot(tokens, up_all, preferred_element_type=jnp.float32)
    hidden = jax.nn.gelu(preact, approximate=False).astype(jnp.bfloat16)
    partial_value = jnp.dot(hidden, down_all, preferred_element_type=jnp.float32).astype(
        jnp.bfloat16
    )
    part = sum_over_cores(partial_value, 1).astype(jnp.bfloat16)
    part = part.reshape(size, patch_rows, part.shape[1])
    mixed = lax.dynamic_index_in_dim(part, place, 0, keepdims=False).astype(jnp.float32)
    for turn in range(1, size):
        pairs = [(base + i, base + (i ^ turn)) for base in range(0, seq, size) for i in range(size)]
        piece = lax.dynamic_index_in_dim(part, lax.bitwise_xor(place, turn), 0, keepdims=False)
        mixed = mixed + lax.ppermute(piece, "seq", pairs).astype(jnp.float32)
    mixed = join_cores(mixed.astype(jnp.bfloat16), 1).astype(jnp.float32)

    kv_in = scale_rows(
        patch_states.astype(jnp.float32) + mixed, kv_gain.astype(jnp.float32)
    ).astype(jnp.bfloat16)
    projected = jnp.dot(kv_in, kv_weight, preferred_element_type=jnp.float32).reshape(
        patch_rows, heads_here, 2, HS
    )
    kv_pack = (
        jnp.stack([unit_rows(projected[:, :, 0]), projected[:, :, 1]], axis=2)
        .astype(jnp.bfloat16)
        .reshape(patch_rows, heads_here * 2 * HS)
    )
    return kv_pack, queries


def on_device(
    patch_states,
    mlp_gain,
    up_weight,
    down_weight,
    kv_gain,
    kv_weight,
    byte_states,
    query_weight,
    out_weight,
    patch_counts,
    byte_patch,
):
    seq = lax.axis_size("seq")
    patch_rows = patch_states.shape[0]
    operands = (
        patch_states, mlp_gain, up_weight, down_weight, kv_gain, kv_weight, byte_states,
        query_weight,
    )
    fewest = patch_rows // 2
    depth = (WIN + fewest - 2) // fewest
    fits = seq == 4 * PLANE and lax.axis_size("mp") == 2 and depth == PLANE
    fits = fits and up_weight.shape[0] % 128 == 0 and up_weight.shape[1] % (PLANE * 128) == 0
    fits = fits and PLANE * patch_rows == patch_states.shape[1] == 2 * kv_weight.shape[1]
    fits = fits and out_weight.shape[1] == kv_weight.shape[1]
    if fits:
        return patch_block(*operands, patch_counts, byte_patch, out_weight, seq // PLANE)
    kv_pack, queries = patch_block_plain(*operands)
    kv_all, counts = [kv_pack], [patch_counts]
    for back in range(1, depth + 1):
        pairs = [(i, i + back) for i in range(max(0, seq - back))]
        kv_all.append(lax.ppermute(kv_pack, "seq", pairs))
        counts.append(lax.ppermute(patch_counts, "seq", pairs))
    kv_all, counts = jnp.stack(kv_all), jnp.concatenate(counts)
    kv_all = kv_all.reshape((depth + 1) * patch_rows, kv_all.shape[2])
    term = attend(queries, byte_patch, counts, kv_all, out_weight)
    return sum_over_cores(term, 0).astype(jnp.bfloat16)


def solution(mesh):
    in_specs = (
        P("seq", None),
        P(),
        P("seq", "mp"),
        P("mp", "seq"),
        P(),
        P(None, "mp"),
        P("seq", None),
        P(None, "mp"),
        P("mp", None),
        P("seq"),
        P("seq"),
    )
    out_specs = P(("seq", "mp"), None)
    return jax.shard_map(
        on_device, mesh=mesh, in_specs=in_specs, out_specs=out_specs, check_vma=False
    )
```

```python
import functools
import math

import jax
import jax.numpy as jnp
from jax import lax
from jax.experimental import pallas as pl
from jax.experimental.pallas import tpu as pltpu
from jax.sharding import PartitionSpec as P

HS = 128
WIN = 1024
KEY_TILE = 256
PLANE = 4
TILE = 128


def scale_rows(values, gain):
    return values * lax.rsqrt(jnp.mean(values * values, axis=-1, keepdims=True) + 1e-05) * gain


def unit_rows(values):
    return values * lax.rsqrt(jnp.mean(values * values, axis=-1, keepdims=True) + 1e-06)


def sum_over_cores(value, scatter_dim):
    count = lax.axis_size("mp")
    if count != 2:
        return lax.psum_scatter(value, "mp", scatter_dimension=scatter_dim, tiled=True).astype(
            jnp.float32
        )
    me = lax.axis_index("mp")
    width = value.shape[scatter_dim] // 2
    theirs = lax.dynamic_slice_in_dim(value, (1 - me) * width, width, scatter_dim)
    mine = lax.dynamic_slice_in_dim(value, me * width, width, scatter_dim)
    got = lax.ppermute(theirs, "mp", [(0, 1), (1, 0)])
    return mine.astype(jnp.float32) + got.astype(jnp.float32)


def join_cores(value, dim):
    count = lax.axis_size("mp")
    if count != 2:
        return lax.all_gather(value, "mp", axis=dim, tiled=True)
    me = lax.axis_index("mp")
    got = lax.ppermute(value, "mp", [(0, 1), (1, 0)])
    first = jnp.where(me == 0, value, got)
    second = jnp.where(me == 0, got, value)
    return jnp.concatenate([first, second], axis=dim)


def one_row(folded):
    return jnp.concatenate([folded[i : i + 1, :] for i in range(folded.shape[0])], axis=1)


def block_kernel(
    patch, mlp_gain, up, down, kv_gain, kv_weight, byte_states, query_weight, count,
    byte_patch_rows, out_weight,
    out,
    kv_out, query_out, count_out, num, den, term_send, term_kept, term_got, byte_patch,
    up_all, down_all, tokens, hidden, core_send, core_got, kept, plane_send, plane_got, mixed,
    swap_send, swap_recv, chunk_recv, right_send, left_send,
    token_send, token_recv, half_send, half_recv,
    core_sems, plane_sems, plane_recv, mixed_send, mixed_recv, local_sems,
    halo_send, halo_recv, count_send, count_recv, term_sems, term_recv,
):
    seq, core = lax.axis_index("seq"), lax.axis_index("mp")
    depth = lax.axis_size("seq") // PLANE
    z, place = seq // PLANE, lax.rem(seq, PLANE)
    y, x = place // 2, lax.rem(place, 2)
    rows, features = patch.shape
    thin = up.shape[0]
    units = up_all.shape[1]
    half = features // 2
    wide = features // (2 * depth)
    MESH = pl.DeviceIdType.MESH

    def member(turn):
        return 2 * lax.rem(y + turn // 2, 2) + lax.rem(x + lax.rem(turn, 2), 2)

    def peer(turn):
        return (z * PLANE + member(turn), core)

    partner = (seq, 1 - core)

    barrier = pltpu.get_barrier_semaphore()
    for turn in range(1, PLANE):
        pl.semaphore_signal(barrier, inc=1, device_id=peer(turn), device_id_type=MESH)
    pl.semaphore_signal(barrier, inc=1, device_id=partner, device_id_type=MESH)

    @pl.when(z > 0)
    def _():
        pl.semaphore_signal(barrier, inc=1, device_id=(seq - PLANE, core), device_id_type=MESH)

    @pl.when(z < depth - 1)
    def _():
        pl.semaphore_signal(barrier, inc=1, device_id=(seq + PLANE, core), device_id_type=MESH)

    pl.semaphore_wait(
        barrier, PLANE + jnp.where(z > 0, 1, 0) + jnp.where(z < depth - 1, 1, 0)
    )

    def remote(src, dst, send, recv, device):
        return pltpu.make_async_remote_copy(
            src_ref=src, dst_ref=dst, send_sem=send, recv_sem=recv, device_id=device,
            device_id_type=MESH,
        )

    def chunk(kind, index):
        if kind == 0:
            return up_all.at[pl.ds(pl.multiple_of(index * thin, thin), thin), :]
        return down_all.at[index]

    def held(kind, owner):
        start = pl.multiple_of(owner * units, units)
        if kind == 0:
            return up.at[:, pl.ds(start, units)]
        return down.at[pl.ds(start, units), :]

    def swap(kind, turn):
        index = z * PLANE + place
        return remote(
            held(kind, member(turn)), chunk(kind, index), swap_send.at[kind, turn],
            swap_recv.at[kind, turn], peer(turn),
        )

    def swap_arrives(kind, turn):
        index = z * PLANE + member(turn)
        return remote(
            chunk(kind, index), chunk(kind, index), swap_send.at[kind, turn],
            swap_recv.at[kind, turn], peer(turn),
        )

    def pass_right(kind, index):
        return remote(
            chunk(kind, index), chunk(kind, index), right_send.at[kind, index],
            chunk_recv.at[kind, index], (seq + PLANE, core),
        )

    def pass_left(kind, index):
        return remote(
            chunk(kind, index), chunk(kind, index), left_send.at[kind, index],
            chunk_recv.at[kind, index], (seq - PLANE, core),
        )

    def spread(kind, index):
        @pl.when(z < depth - 1)
        def _():
            pass_right(kind, index).start()

        @pl.when(z > 0)
        def _():
            pass_left(kind, index).start()

    def hop(kind, step):
        far, turn = step // PLANE, lax.rem(step, PLANE)

        @pl.when(z - 1 - far >= 0)
        def _():
            index = (z - 1 - far) * PLANE + member(turn)
            pass_left(kind, index).wait_recv()

            @pl.when(z < depth - 1)
            def _():
                pass_right(kind, index).start()

        @pl.when(z + 1 + far < depth)
        def _():
            index = (z + 1 + far) * PLANE + member(turn)
            pass_right(kind, index).wait_recv()

            @pl.when(z > 0)
            def _():
                pass_left(kind, index).start()

    own = [
        pltpu.make_async_copy(held(kind, place), chunk(kind, seq), local_sems.at[kind])
        for kind in range(2)
    ]
    for kind in range(2):
        own[kind].start()
    for turn in range(1, PLANE):
        swap(0, turn).start()
    for kind in range(2):
        own[kind].wait()
        spread(kind, seq)

    def later(turn):
        return member(turn) > place

    def source(turn):
        return jnp.where(later(turn), 0, PLANE)

    def distance(turn):
        return lax.rem(member(turn) - place + PLANE, PLANE)

    def from_distance(turn):
        return lax.rem(place - member(turn) + PLANE, PLANE)

    def count_on():
        return remote(
            count_out.at[0], count_out.at[PLANE], count_send.at[0], count_recv.at[0],
            (seq + PLANE, core),
        )

    def count_over(turn):
        return remote(
            count_out.at[source(turn)], count_out.at[distance(turn)], count_send.at[turn],
            count_recv.at[turn], peer(turn),
        )

    def count_arrives(turn):
        part = count_out.at[from_distance(turn)]
        return remote(part, part, count_send.at[turn], count_recv.at[turn], peer(turn))

    def count_chain():
        @pl.when(z > 0)
        def _():
            count_on().wait_recv()

        for turn in range(1, PLANE):
            @pl.when(later(turn) | (z > 0))
            def _(turn=turn):
                count_over(turn).start()

    count_out[0] = count[...]
    num[...] = jnp.zeros_like(num)
    den[...] = jnp.zeros_like(den)
    turned = jnp.transpose(byte_patch_rows[...])
    for i in range(byte_patch_rows.shape[0]):
        byte_patch[i * 128 : (i + 1) * 128, :] = turned[:, i : i + 1]

    @pl.when(z < depth - 1)
    def _():
        count_on().start()

    def piece(step):
        return pl.ds(pl.multiple_of(step * TILE, TILE), TILE)

    def halo_on(step):
        return remote(
            kv_out.at[0, piece(step), :], kv_out.at[PLANE, piece(step), :],
            halo_send.at[0, step], halo_recv.at[0, step], (seq + PLANE, core),
        )

    def halo_over(turn, step):
        return remote(
            kv_out.at[source(turn), piece(step), :], kv_out.at[distance(turn), piece(step), :],
            halo_send.at[turn, step], halo_recv.at[turn, step], peer(turn),
        )

    def halo_arrives(turn, step):
        part = kv_out.at[from_distance(turn), piece(step), :]
        return remote(part, part, halo_send.at[turn, step], halo_recv.at[turn, step], peer(turn))

    gain = one_row(mlp_gain[...].astype(jnp.float32))
    row_start = pl.multiple_of(place * rows, rows)

    @pl.loop(0, rows // TILE)
    def _(tile):
        low = pl.multiple_of(tile * TILE, TILE)
        values = patch[pl.ds(low, TILE), :].astype(jnp.float32)
        tokens[pl.ds(row_start + low, TILE), :] = scale_rows(values, gain).astype(jnp.bfloat16)

    for turn in range(1, PLANE):
        swap_arrives(0, turn).wait_recv()
        spread(0, z * PLANE + member(turn))
    for turn in range(1, PLANE):
        swap(1, turn).start()

    def token_part(owner, side):
        return tokens.at[
            pl.ds(pl.multiple_of(owner * rows, rows), rows),
            pl.ds(pl.multiple_of(side * half, half), half),
        ]

    def send_tokens(turn):
        return remote(
            token_part(place, core), token_part(place, core), token_send.at[turn],
            token_recv.at[turn], peer(turn),
        )

    def tokens_arrive(turn):
        part = token_part(member(turn), core)
        return remote(part, part, token_send.at[turn], token_recv.at[turn], peer(turn))

    def half_over(turn):
        part = token_part(member(turn), core)
        return remote(part, part, half_send.at[turn], half_recv.at[turn], partner)

    def half_arrives(turn):
        part = token_part(member(turn), 1 - core)
        return remote(part, part, half_send.at[turn], half_recv.at[turn], partner)

    for turn in range(1, PLANE):
        send_tokens(turn).start()

    heads = query_weight.shape[1] // HS
    query_rows = byte_states.shape[0] // PLANE

    @pl.loop(0, PLANE)
    def _(step):
        low = pl.multiple_of(step * query_rows, query_rows)
        product = jnp.dot(
            byte_states[pl.ds(low, query_rows), :], query_weight[...],
            preferred_element_type=jnp.float32,
        )
        for head in range(heads):
            columns = slice(head * HS, (head + 1) * HS)
            query_out[pl.ds(low, query_rows), columns] = unit_rows(product[:, columns]).astype(
                jnp.bfloat16
            )
        hop(0, step)

    count_chain()
    for turn in range(1, PLANE):
        swap_arrives(1, turn).wait_recv()
        spread(1, z * PLANE + member(turn))

    @pl.loop(PLANE, 2 * PLANE)
    def _(step):
        hop(0, step)

    for turn in range(1, PLANE):
        tokens_arrive(turn).wait_recv()
        half_over(turn).start()

    @pl.loop(2 * PLANE, (depth - 1) * PLANE)
    def _(step):
        hop(0, step)

    for turn in range(1, PLANE):
        half_arrives(turn).wait_recv()

    tall = PLANE * rows // (2 * PLANE)

    @pl.loop(0, 2 * PLANE)
    def _(step):
        low = pl.multiple_of(step * tall, tall)
        preact = jnp.dot(
            tokens[pl.ds(low, tall), :], up_all[...], preferred_element_type=jnp.float32
        )
        gelu = 0.5 * preact * (1.0 + lax.erf(preact * math.sqrt(0.5)))
        hidden[pl.ds(low, tall), :] = gelu.astype(jnp.bfloat16)
        hop(1, step)

    for turn in range(1, PLANE):
        send_tokens(turn).wait_send()
        half_over(turn).wait_send()
    kv_held = tokens.at[:, 0:half]
    out_held = tokens.at[0 : out_weight.shape[0], half : 2 * half]
    kv_load = pltpu.make_async_copy(kv_weight, kv_held, local_sems.at[0])
    out_load = pltpu.make_async_copy(out_weight, out_held, local_sems.at[1])
    kv_load.start()
    out_load.start()

    near = jnp.minimum(z, depth - 1 - z)

    def order(turn):
        swapped = jnp.where((near == 1) & (turn < 2), 1 - turn, turn)
        return jnp.where(z < depth // 2, swapped, depth - 1 - swapped)

    def plane_out(turn, to):
        start = pl.multiple_of(member(to) * rows, rows)
        return remote(
            plane_send.at[turn, pl.ds(start, rows), :], plane_got.at[turn, to - 1],
            plane_sems.at[turn, to], plane_recv.at[turn, to], peer(to),
        )

    def core_swap(turn):
        return remote(
            core_send, core_got.at[turn], core_sems.at[0, turn], core_sems.at[1, turn], partner
        )

    def product(turn, side, out):
        chunks = order(turn) * PLANE + side * (PLANE // 2)
        weight = jnp.concatenate([down_all[chunks + i] for i in range(PLANE // 2)], axis=1)

        @pl.loop(0, PLANE)
        def _(owner):
            low = pl.multiple_of(owner * rows, rows)
            out[pl.ds(low, rows), :] = jnp.dot(
                hidden[pl.ds(low, rows), :], weight, preferred_element_type=jnp.float32
            ).astype(jnp.bfloat16)

    def one_block(turn):
        product(turn, 1 - core, core_send)
        core_swap(turn).start()
        product(turn, core, kept)
        core_swap(turn).wait()

        @pl.loop(0, PLANE)
        def _(owner):
            low = pl.multiple_of(owner * rows, rows)
            total = kept[pl.ds(low, rows), :].astype(jnp.float32) + core_got[
                turn, pl.ds(low, rows), :
            ].astype(jnp.float32)
            plane_send[turn, pl.ds(low, rows), :] = total.astype(jnp.bfloat16)

        for to in range(1, PLANE):
            plane_out(turn, to).start()

    @pl.loop(0, depth - 1)
    def _(turn):
        one_block(turn)

    @pl.loop(2 * PLANE, (depth - 1) * PLANE)
    def _(step):
        hop(1, step)

    one_block(depth - 1)

    def mixed_over(turn, side):
        part = mixed.at[2 * order(turn) + side]
        return remote(part, part, mixed_send.at[turn], mixed_recv.at[turn], partner)

    @pl.loop(0, depth)
    def _(turn):
        total = plane_send[turn, pl.ds(row_start, rows), :].astype(jnp.float32)
        for to in range(1, PLANE):
            plane_out(turn, to).wait_recv()
            total = total + plane_got[turn, to - 1].astype(jnp.float32)
        mixed[2 * order(turn) + core] = total.astype(jnp.bfloat16)
        mixed_over(turn, core).start()

    @pl.loop(0, depth)
    def _(turn):
        mixed_over(turn, 1 - core).wait_recv()

    kv_load.wait()
    out_load.wait()
    later_gain = one_row(kv_gain[...].astype(jnp.float32))

    @pl.loop(0, rows // TILE)
    def _(tile):
        low = pl.multiple_of(tile * TILE, TILE)
        more = jnp.concatenate(
            [mixed[i, pl.ds(low, TILE), :] for i in range(2 * depth)], axis=1
        )
        values = patch[pl.ds(low, TILE), :].astype(jnp.float32) + more.astype(jnp.float32)
        kv_in = scale_rows(values, later_gain).astype(jnp.bfloat16)
        projected = jnp.dot(kv_in, kv_held[...], preferred_element_type=jnp.float32)
        for head in range(heads):
            key = slice(head * 2 * HS, head * 2 * HS + HS)
            value = slice(head * 2 * HS + HS, (head + 1) * 2 * HS)
            kv_out[0, pl.ds(low, TILE), key] = unit_rows(projected[:, key]).astype(jnp.bfloat16)
            kv_out[0, pl.ds(low, TILE), value] = projected[:, value].astype(jnp.bfloat16)

        @pl.when(z < depth - 1)
        def _():
            halo_on(tile).start()

        for turn in range(1, PLANE - 1):
            @pl.when(later(turn))
            def _(turn=turn):
                halo_over(turn, tile).start()

    @pl.when(later(PLANE - 1))
    def _():
        @pl.loop(0, rows // TILE)
        def _(step):
            halo_over(PLANE - 1, step).start()

    scale = 2.0 / math.sqrt(HS) * math.log2(math.e)
    byte_rows = byte_patch.shape[0] // PLANE

    def attend_tile(slot, tile):
        low = pl.multiple_of(tile * byte_rows, byte_rows)
        here = pl.ds(low, byte_rows)
        live = count_out[slot][0:1, 0:1]
        before = jnp.zeros((1, 1), jnp.int32)
        for back in range(1, PLANE + 1):
            before = before + jnp.where(slot >= back, count_out[back][0:1, 0:1], 0)
        mine = byte_patch[here, :] + before
        for start in range(0, rows, KEY_TILE):
            position = start + lax.broadcasted_iota(jnp.int32, (byte_rows, KEY_TILE), 1)
            gap = mine - position
            usable = (position < live) & (gap >= 0) & (gap < WIN)
            keys = slice(start, start + KEY_TILE)
            scores = [
                lax.dot_general(
                    query_out[here, head * HS : (head + 1) * HS],
                    kv_out[slot, keys, head * 2 * HS : head * 2 * HS + HS],
                    (((1,), (1,)), ((), ())),
                    preferred_element_type=jnp.float32,
                )
                for head in range(heads)
            ]
            weights = [jnp.where(usable, jnp.exp2(score * scale), 0.0) for score in scores]
            for head in range(heads):
                columns = slice(head * HS, (head + 1) * HS)
                weight = weights[head]
                den[here, columns] += weight[:, :HS] + weight[:, HS:]
                num[here, columns] += jnp.dot(
                    weight.astype(jnp.bfloat16),
                    kv_out[slot, keys, head * 2 * HS + HS : (head + 1) * 2 * HS],
                    preferred_element_type=jnp.float32,
                )

    @pl.loop(0, PLANE)
    def _(step):
        @pl.when(z > 0)
        def _():
            halo_on(step).wait_recv()
            for turn in range(1, PLANE - 1):
                @pl.when(member(turn) < place)
                def _(turn=turn):
                    halo_over(turn, step).start()

        attend_tile(0, step)

    @pl.when((z > 0) & (member(PLANE - 1) < place))
    def _():
        @pl.loop(0, rows // TILE)
        def _(step):
            halo_over(PLANE - 1, step).start()

    for turn in range(1, PLANE):
        @pl.when((member(turn) < place) | (z > 0))
        def _(turn=turn):
            count_arrives(turn).wait_recv()

    @pl.when(z > 0)
    def _():
        @pl.loop(0, PLANE)
        def _(tile):
            attend_tile(PLANE, tile)

    @pl.loop(1, PLANE)
    def _(turn):
        @pl.when((member(turn) < place) | (z > 0))
        def _():
            @pl.loop(0, rows // TILE)
            def _(step):
                halo_arrives(turn, step).wait_recv()

            @pl.loop(0, PLANE)
            def _(tile):
                attend_tile(from_distance(turn), tile)

    def finish(tile):
        low = pl.multiple_of(tile * byte_rows, byte_rows)
        parts = []
        for head in range(heads):
            columns = slice(head * HS, (head + 1) * HS)
            total = jnp.sum(den[pl.ds(low, byte_rows), columns], axis=1, keepdims=True)
            parts.append((num[pl.ds(low, byte_rows), columns] / total).astype(jnp.bfloat16))
        return jnp.dot(
            jnp.concatenate(parts, axis=1), out_held[...], preferred_element_type=jnp.float32
        ).astype(jnp.bfloat16)

    pair = PLANE // 2

    def term_over(tile):
        return remote(
            term_send.at[tile], term_got.at[tile], term_sems.at[tile], term_recv.at[tile], partner
        )

    @pl.loop(0, pair)
    def _(tile):
        term_send[tile] = finish((1 - core) * pair + tile)
        term_over(tile).start()

    @pl.loop(0, pair)
    def _(tile):
        term_kept[tile] = finish(core * pair + tile)

    @pl.loop(0, pair)
    def _(tile):
        term_over(tile).wait()
        total = term_kept[tile].astype(jnp.float32) + term_got[tile].astype(jnp.float32)
        out[pl.ds(pl.multiple_of(tile * byte_rows, byte_rows), byte_rows), :] = total.astype(
            jnp.bfloat16
        )

    for turn in range(1, PLANE):
        @pl.when(later(turn) | (z > 0))
        def _(turn=turn):
            count_over(turn).wait_send()

            @pl.loop(0, rows // TILE)
            def _(step):
                halo_over(turn, step).wait_send()

    @pl.when(z < depth - 1)
    def _():
        count_on().wait_send()

        @pl.loop(0, rows // TILE)
        def _(step):
            halo_on(step).wait_send()

    for turn in range(1, PLANE):
        for kind in range(2):
            swap(kind, turn).wait_send()

    @pl.loop(0, depth)
    def _(turn):
        for to in range(1, PLANE):
            plane_out(turn, to).wait_send()
        mixed_over(turn, core).wait_send()

    @pl.loop(0, depth * PLANE)
    def _(index):
        @pl.when((z < depth - 1) & (index // PLANE <= z))
        def _():
            for kind in range(2):
                pass_right(kind, index).wait_send()

        @pl.when((z > 0) & (index // PLANE >= z))
        def _():
            for kind in range(2):
                pass_left(kind, index).wait_send()


def patch_block(
    patch, mlp_gain, up, down, kv_gain, kv_weight, byte_states, query_weight, count,
    byte_patch, out_weight, depth
):
    rows, features = patch.shape
    thin = up.shape[0]
    units = up.shape[1] // PLANE
    wide = features // (2 * depth)
    bytes_here, width = byte_states.shape[0], out_weight.shape[1]
    vmem = pl.BlockSpec(memory_space=pltpu.VMEM)
    hbm = pl.BlockSpec(memory_space=pl.ANY)
    bf16 = lambda *shape: pltpu.VMEM(shape, jnp.bfloat16)
    dma = lambda *shape: pltpu.SemaphoreType.DMA(shape)
    return pl.pallas_call(
        block_kernel,
        in_specs=[vmem] * 5 + [hbm] + [vmem] * 4 + [hbm],
        out_specs=vmem,
        out_shape=jax.ShapeDtypeStruct((bytes_here // 2, width), jnp.bfloat16),
        scratch_shapes=[
            bf16(PLANE + 1, rows, kv_weight.shape[1]),
            bf16(bytes_here, query_weight.shape[1]),
            pltpu.VMEM((PLANE + 1, 8, 128), jnp.int32),
            pltpu.VMEM((bytes_here, query_weight.shape[1]), jnp.float32),
            pltpu.VMEM((bytes_here, query_weight.shape[1]), jnp.float32),
            bf16(2, bytes_here // 4, width),
            bf16(2, bytes_here // 4, width),
            bf16(2, bytes_here // 4, width),
            pltpu.VMEM((bytes_here, 1), jnp.int32),
            bf16(features, units),
            bf16(depth * PLANE, units, thin),
            bf16(PLANE * rows, features),
            bf16(PLANE * rows, units),
            bf16(PLANE * rows, wide),
            bf16(depth, PLANE * rows, wide),
            bf16(PLANE * rows, wide),
            bf16(depth, PLANE * rows, wide),
            bf16(depth, PLANE - 1, rows, wide),
            bf16(2 * depth, rows, wide),
            dma(2, PLANE), dma(2, PLANE), dma(2, depth * PLANE),
            dma(2, depth * PLANE), dma(2, depth * PLANE),
            dma(PLANE), dma(PLANE), dma(PLANE), dma(PLANE),
            dma(2, depth), dma(depth, PLANE), dma(depth, PLANE), dma(depth), dma(depth), dma(2),
            dma(PLANE, rows // TILE), dma(PLANE, rows // TILE), dma(PLANE), dma(PLANE),
            dma(2), dma(2),
        ],
        compiler_params=pltpu.CompilerParams(
            collective_id=0, has_side_effects=True, vmem_limit_bytes=60 * 2**20
        ),
        cost_estimate=pl.CostEstimate(
            flops=40 * 10**9, bytes_accessed=60 * 10**6, transcendentals=0
        ),
    )(
        patch, mlp_gain.reshape(-1, 128), up, down, kv_gain.reshape(-1, 128), kv_weight, byte_states, query_weight,
        jnp.broadcast_to(count, (8, 128)), byte_patch.reshape(-1, 128), out_weight,
    )


def attend_kernel(
    heads, blocks, counts, by_byte, query, byte_patch, kv, out_weight, out, num, den
):
    num[...] = jnp.zeros_like(num)
    den[...] = jnp.zeros_like(den)
    me = lax.axis_index("seq")
    rows = query.shape[0]
    tile = pl.program_id(0)
    lowest, highest = by_byte[tile * rows], by_byte[tile * rows + rows - 1]
    scale = 2.0 / math.sqrt(HS) * math.log2(math.e)
    slots = kv.shape[0] // blocks
    first = jnp.int32(0)
    for back in range(blocks):
        live = jnp.where(me >= back, counts[back], 0)
        if back:
            first = first - live
        for low in range(0, slots, KEY_TILE):
            last = first + jnp.minimum(live, low + KEY_TILE) - 1
            seen = (low < live) & (first + low <= highest) & (last > lowest - WIN)

            @pl.when(seen)
            def _(start=back * slots + low, low=low, first=first, live=live):
                position = low + lax.broadcasted_iota(jnp.int32, (rows, KEY_TILE), 1)
                gap = byte_patch[...] - first - position
                usable = (position < live) & (gap >= 0) & (gap < WIN)
                keys = slice(start, start + KEY_TILE)
                for head in range(heads):
                    columns = slice(head * HS, (head + 1) * HS)
                    scores = lax.dot_general(
                        query[:, columns],
                        kv[keys, head * 2 * HS : head * 2 * HS + HS],
                        (((1,), (1,)), ((), ())),
                        preferred_element_type=jnp.float32,
                    )
                    weights = jnp.where(usable, jnp.exp2(scores * scale), 0.0)
                    den[:, columns] += weights[:, :HS] + weights[:, HS:]
                    num[:, columns] += jnp.dot(
                        weights.astype(jnp.bfloat16),
                        kv[keys, head * 2 * HS + HS : (head + 1) * 2 * HS],
                        preferred_element_type=jnp.float32,
                    )

    parts = []
    for head in range(heads):
        columns = slice(head * HS, (head + 1) * HS)
        total = jnp.sum(den[:, columns], axis=1, keepdims=True)
        parts.append((num[:, columns] / total).astype(jnp.bfloat16))
    out[...] = jnp.dot(
        jnp.concatenate(parts, axis=1), out_weight[...], preferred_element_type=jnp.float32
    ).astype(jnp.bfloat16)


def attend(query, byte_patch, counts, kv, out_weight):
    rows, width = query.shape
    tile = min(256, rows)
    blocks = counts.shape[0]
    smem = pl.BlockSpec(memory_space=pltpu.SMEM)
    tiled = lambda columns: pl.BlockSpec((tile, columns), lambda i: (i, 0))
    whole = lambda array: pl.BlockSpec(array.shape, lambda i: (0, 0))
    return pl.pallas_call(
        functools.partial(attend_kernel, width // HS, blocks),
        grid=(rows // tile,),
        in_specs=[smem, smem, tiled(width), tiled(1), whole(kv), whole(out_weight)],
        out_specs=tiled(out_weight.shape[1]),
        out_shape=jax.ShapeDtypeStruct((rows, out_weight.shape[1]), jnp.bfloat16),
        scratch_shapes=[pltpu.VMEM((tile, width), jnp.float32)] * 2,
        compiler_params=pltpu.CompilerParams(vmem_limit_bytes=48 * 2**20),
        cost_estimate=pl.CostEstimate(
            flops=4 * rows * kv.shape[0] * width, bytes_accessed=4 * kv.size, transcendentals=0
        ),
    )(counts, byte_patch, query, byte_patch[:, None], kv, out_weight)


def patch_block_plain(
    patch_states, mlp_gain, up_weight, down_weight, kv_gain, kv_weight, byte_states, query_weight
):
    seq = lax.axis_size("seq")
    patch_rows = patch_states.shape[0]
    size = PLANE if seq % PLANE == 0 else 1
    groups = [[base + i for i in range(size)] for base in range(0, seq, size)]
    across = [[base + i for base in range(0, seq, size)] for i in range(size)]
    place = lax.rem(lax.axis_index("seq"), size)

    up_part = lax.all_to_all(up_weight, "seq", 1, 0, axis_index_groups=groups, tiled=True)
    down_part = lax.all_to_all(down_weight, "seq", 0, 1, axis_index_groups=groups, tiled=True)
    up_all = lax.all_gather(up_part, "seq", axis=0, tiled=True, axis_index_groups=across)
    down_all = lax.all_gather(down_part, "seq", axis=1, tiled=True, axis_index_groups=across)

    normed = scale_rows(patch_states.astype(jnp.float32), mlp_gain.astype(jnp.float32)).astype(
        jnp.bfloat16
    )
    tokens = lax.all_gather(normed, "seq", axis=0, tiled=True, axis_index_groups=groups)
    heads_here = kv_weight.shape[1] // (2 * HS)
    bytes_here = byte_states.shape[0]
    query_proj = jnp.dot(byte_states, query_weight, preferred_element_type=jnp.float32).reshape(
        bytes_here, heads_here, HS
    )
    queries = unit_rows(query_proj).astype(jnp.bfloat16).reshape(bytes_here, heads_here * HS)

    preact = jnp.dot(tokens, up_all, preferred_element_type=jnp.float32)
    hidden = jax.nn.gelu(preact, approximate=False).astype(jnp.bfloat16)
    partial_value = jnp.dot(hidden, down_all, preferred_element_type=jnp.float32).astype(
        jnp.bfloat16
    )
    part = sum_over_cores(partial_value, 1).astype(jnp.bfloat16)
    part = part.reshape(size, patch_rows, part.shape[1])
    mixed = lax.dynamic_index_in_dim(part, place, 0, keepdims=False).astype(jnp.float32)
    for turn in range(1, size):
        pairs = [(base + i, base + (i ^ turn)) for base in range(0, seq, size) for i in range(size)]
        piece = lax.dynamic_index_in_dim(part, lax.bitwise_xor(place, turn), 0, keepdims=False)
        mixed = mixed + lax.ppermute(piece, "seq", pairs).astype(jnp.float32)
    mixed = join_cores(mixed.astype(jnp.bfloat16), 1).astype(jnp.float32)

    kv_in = scale_rows(
        patch_states.astype(jnp.float32) + mixed, kv_gain.astype(jnp.float32)
    ).astype(jnp.bfloat16)
    projected = jnp.dot(kv_in, kv_weight, preferred_element_type=jnp.float32).reshape(
        patch_rows, heads_here, 2, HS
    )
    kv_pack = (
        jnp.stack([unit_rows(projected[:, :, 0]), projected[:, :, 1]], axis=2)
        .astype(jnp.bfloat16)
        .reshape(patch_rows, heads_here * 2 * HS)
    )
    return kv_pack, queries


def on_device(
    patch_states,
    mlp_gain,
    up_weight,
    down_weight,
    kv_gain,
    kv_weight,
    byte_states,
    query_weight,
    out_weight,
    patch_counts,
    byte_patch,
):
    seq = lax.axis_size("seq")
    patch_rows = patch_states.shape[0]
    operands = (
        patch_states, mlp_gain, up_weight, down_weight, kv_gain, kv_weight, byte_states,
        query_weight,
    )
    fewest = patch_rows // 2
    depth = (WIN + fewest - 2) // fewest
    fits = seq == 4 * PLANE and lax.axis_size("mp") == 2 and depth == PLANE
    fits = fits and up_weight.shape[0] % 128 == 0 and up_weight.shape[1] % (PLANE * 128) == 0
    fits = fits and PLANE * patch_rows == patch_states.shape[1] == 2 * kv_weight.shape[1]
    fits = fits and out_weight.shape[1] == kv_weight.shape[1] and byte_patch.shape[0] == 1024
    if fits:
        return patch_block(*operands, patch_counts, byte_patch, out_weight, seq // PLANE)
    kv_pack, queries = patch_block_plain(*operands)
    kv_all, counts = [kv_pack], [patch_counts]
    for back in range(1, depth + 1):
        pairs = [(i, i + back) for i in range(max(0, seq - back))]
        kv_all.append(lax.ppermute(kv_pack, "seq", pairs))
        counts.append(lax.ppermute(patch_counts, "seq", pairs))
    kv_all, counts = jnp.stack(kv_all), jnp.concatenate(counts)
    kv_all = kv_all.reshape((depth + 1) * patch_rows, kv_all.shape[2])
    term = attend(queries, byte_patch, counts, kv_all, out_weight)
    return sum_over_cores(term, 0).astype(jnp.bfloat16)


def solution(mesh):
    in_specs = (
        P("seq", None),
        P(),
        P("seq", "mp"),
        P("mp", "seq"),
        P(),
        P(None, "mp"),
        P("seq", None),
        P(None, "mp"),
        P("mp", None),
        P("seq"),
        P("seq"),
    )
    out_specs = P(("seq", "mp"), None)
    return jax.shard_map(
        on_device, mesh=mesh, in_specs=in_specs, out_specs=out_specs, check_vma=False
    )
```
